256 devices in a mesh: lon: 16 (over y, x), lat: 8 (over z), depth: 2 (over core).
Axes of the slice: x: 4, y: 4, z: 8, core: 2. Of those that a mesh axis runs over, the one named last changes fastest.
Arguments:
- states: float32 [4, 20, 256, 4096], P(None, 'depth', 'lat', 'lon'), may hold values from -2.5 to 2.5
- direction: float32 [20, 256, 4096], P('depth', 'lat', 'lon'), may hold values from -6 to 6
- mixing: float32 [20, 256, 4096], P('depth', 'lat', 'lon'), may hold values from 0.3 to 1
- level_dz: float32 [20], P('depth'), may hold values from 0.5 to 2
- lat_width: float32 [256], P('lat'), may hold values from 0.5 to 2
- cost_weight: float32 [20, 256], P(None, 'lat'), may hold values from 0.1 to 1
- ocean_columns: int32 [256, 4096], P('lat', 'lon'), may hold values 0 or 1
- atlantic: int32 [256, 4096], P('lat', 'lon'), may hold values 0 or 1
- levels: int32 [256, 4096], P('lat', 'lon'), may hold values from 4 to 20
Outputs:
- hessian_product: float32 [20, 256, 4096], P('depth', 'lat', 'lon')
- gradient: float32 [20, 256, 4096], P('depth', 'lat', 'lon')
- overturning: float32 [20, 256], P('depth', 'lat')
The draws below stay inside these ranges and needn't reach their ends.
All inputs are finite; a program needn't handle non-finite values. No bound on the sum of `ocean_columns` or of `atlantic` on one device may be relied on, other than what follows from the above.
Results may differ from the reference program's by a relative error of at most 0.00002.
Values sent between devices are 32-bit elements; how exact they have to be, the bound alone decides.
A program may use at most 64 MiB of HBM per device.

```python
import math
import jax
import jax.numpy as jnp
from jax import lax

STEPS = 4
NK = 20
NLAT = 256
NLON = 4096


def touch_ends(entries, key, low, top_value):
    index_at = [jax.random.randint(jax.random.fold_in(key, axis), (), 0, length) for axis, length in enumerate(entries.shape)]
    widest = entries.shape.index(max(entries.shape))
    next_to = index_at[:widest] + [(index_at[widest] + 1) % entries.shape[widest]] + index_at[widest + 1:]
    return entries.at[tuple(index_at)].set(low).at[tuple(next_to)].set(top_value)


def steps_of(key, dims, cuts, low, largest):
    def one(axis_at, shards_of):
        steps = jax.random.uniform(jax.random.fold_in(jax.random.fold_in(key, 6), axis_at), (shards_of,), jnp.float32, low / len(cuts), largest / len(cuts))
        return jnp.repeat(jnp.exp(steps), dims[axis_at] // shards_of).reshape((-1,) + (1,) * (len(dims) - axis_at - 1))

    loudness = one(*cuts[0])
    for cut in cuts[1:]:
        loudness = loudness * one(*cut)
    return loudness


def noise(own_key, dims, scale, limit, shards=(), kind=jnp.bfloat16):
    factor_of = steps_of(own_key, dims, shards, -0.22, 0.18) if shards else 1.0
    array = jax.random.normal(own_key, dims, jnp.float32) * scale * factor_of
    return jnp.minimum(jnp.maximum(array, -limit), limit).astype(kind)


def setup_inputs(seed: int = 0) -> dict:
    streams_of = jax.random.split(jax.random.key(seed), 10)
    states = noise(streams_of[0], (STEPS, NK, NLAT, NLON), 0.5, 2.5, ((1, 2), (2, 8), (3, 16)), jnp.float32)
    direction = noise(streams_of[1], (NK, NLAT, NLON), 1.0, 6.0, ((0, 2), (1, 8), (2, 16)), jnp.float32)
    mixing = jnp.clip(jnp.exp(math.log(1.0) - 1.2039728 * jax.random.uniform(streams_of[2], (NK, NLAT, NLON), jnp.float32) ** steps_of(streams_of[2], (NK, NLAT, NLON), ((0, 2), (1, 8), (2, 16)), -0.2, 0.2)), 0.3, 1.0)
    level_dz = jnp.clip(jnp.exp(math.log(2.0) - 1.3862944 * jax.random.uniform(streams_of[3], (NK,), jnp.float32) ** steps_of(streams_of[3], (NK,), ((0, 2),), -0.2, 0.2)), 0.5, 2.0)
    lat_width = jnp.clip(jnp.exp(math.log(2.0) - 1.3862944 * jax.random.uniform(streams_of[4], (NLAT,), jnp.float32) ** steps_of(streams_of[4], (NLAT,), ((0, 8),), -0.2, 0.2)), 0.5, 2.0)
    cost_weight = jnp.clip(jnp.exp(math.log(1.0) - 2.3025851 * jax.random.uniform(streams_of[5], (NK, NLAT), jnp.float32) ** steps_of(streams_of[5], (NK, NLAT), ((1, 8),), -0.2, 0.2)), 0.1, 1.0)
    ocean_columns = touch_ends((jax.random.randint(streams_of[6], (NLAT, NLON), 0, 10) < 9).astype(jnp.int32), jax.random.fold_in(streams_of[6], 1), 0, 1)
    atlantic = touch_ends((jax.random.randint(streams_of[7], (NLAT, NLON), 0, 2) < 1).astype(jnp.int32), jax.random.fold_in(streams_of[7], 1), 0, 1)
    levels = touch_ends(jax.random.randint(streams_of[8], (NLAT, NLON), NK // 5, NK + 1), jax.random.fold_in(streams_of[8], 1), NK // 5, NK).astype(jnp.int32)
    return dict(states=states, direction=direction, mixing=mixing, level_dz=level_dz, lat_width=lat_width, cost_weight=cost_weight, ocean_columns=ocean_columns, atlantic=atlantic, levels=levels)


diffusion_step = 0.08
cubic_drag = 0.15

def neighbours(field_pad, couple_pad):
    centre = field_pad[1:-1, 1:-1, 1:-1]
    summed = jnp.zeros_like(centre)
    for which in range(3):
        for offset in (0, 2):
            window = [slice(1, -1), slice(1, -1), slice(1, -1)]
            window[which] = slice(offset, offset + centre.shape[which])
            window = tuple(window)
            summed = summed + couple_pad[window] * (field_pad[window] - centre)
    return couple_pad[1:-1, 1:-1, 1:-1] * summed

def reference(states, direction, mixing, level_dz, lat_width, cost_weight, ocean_columns, atlantic, levels):
    level_index = jnp.arange(NK, dtype=jnp.int32)[:, None, None]
    wetness = (ocean_columns[None] * (level_index < levels[None]).astype(jnp.int32)).astype(jnp.float32)
    coupling = mixing * wetness
    couple_pad = jnp.pad(coupling, 1)
    area = atlantic.astype(jnp.float32)[None] * level_dz[:, None, None] * lat_width[None, :, None] * (1.0 / math.sqrt(NLON * NK))
    last = states[STEPS - 1]
    final = wetness * (last + diffusion_step * neighbours(jnp.pad(last, 1), couple_pad) - cubic_drag * last * last * last)
    tangent = direction
    tangents = []
    for number in range(STEPS):
        tangents.append(tangent)
        saved = states[number]
        tangent = wetness * (tangent + diffusion_step * neighbours(jnp.pad(tangent, 1), couple_pad) - 3.0 * cubic_drag * saved * saved * tangent)
    zonal = jnp.stack([lax.optimization_barrier(jnp.sum(area * final, axis=2)), lax.optimization_barrier(jnp.sum(area * tangent, axis=2))])
    stream = jnp.flip(jnp.cumsum(jnp.flip(zonal, 1), axis=1), 1)
    forcing = cost_weight[None] * stream * math.sqrt(NLON)
    prefix = jnp.cumsum(forcing, axis=1)
    lam = area * prefix[0][:, :, None]
    tan_adj = area * prefix[1][:, :, None]
    for number in reversed(range(STEPS)):
        saved = states[number]
        damping = 3.0 * cubic_drag * saved * saved
        new_adj = wetness * (tan_adj + diffusion_step * neighbours(jnp.pad(tan_adj, 1), couple_pad) - damping * tan_adj) - 6.0 * cubic_drag * wetness * saved * tangents[number] * lam
        lam = wetness * (lam + diffusion_step * neighbours(jnp.pad(lam, 1), couple_pad) - damping * lam)
        tan_adj = new_adj
    return (tan_adj, lam, stream[0])
```

```python
import functools
import math

import jax
import jax.numpy as jnp
from jax import lax
from jax.experimental import pallas as pl
from jax.experimental.pallas import tpu as pltpu
from jax.sharding import PartitionSpec as P

MESH = pl.DeviceIdType.MESH
diffusion_step = 0.08
cubic_drag = 0.15

HALO = 4


def stencil(couple, value, level, levels):
    here = couple[level] * value[level]
    return around(here, couple[level - 1] * value[level - 1] if level else None, couple[level + 1] * value[level + 1])


def around(here, before, after):
    rows, columns = here.shape
    total = pltpu.roll(here, 1, 1) + pltpu.roll(here, columns - 1, 1)
    total = total + (pltpu.roll(here, 1, 0) + pltpu.roll(here, rows - 1, 0))
    total = total + (after if before is None else before + after)
    return total


def kernel(
    n_lon, n_lat, n_depth, scale, grid_scale,
    states, direction, mixing, level_dz, lat_width, cost_weight, ocean, atlantic, levels_in,
    hess, grad, overturning,
    st_states, st_dir, st_mix, st_ocean, st_atl, st_lev,
    fields, capacity, tan1, tan2, tan3, tan4, tan3_wide, lam, mu,
    flat, strips_out, strips_in, strip3_out, strip3_in, dz_out, dz_in, zone, zones, totals, prefixes, weights,
    in_sem, lat_send, lat_recv, lon_send, lon_recv, diag_send, diag_recv, dep_send, dep_recv,
    zone_send, zone_recv, tot_send, tot_recv, t3_send, t3_recv,
):
    layers, rows, columns = direction.shape
    all_layers = 2 * layers
    ext_rows, ext_columns = fields.shape[-2:]
    lon, lat, dep = lax.axis_index("lon"), lax.axis_index("lat"), lax.axis_index("depth")
    wrap = lambda value, size: lax.rem(value + size, size)

    def at(dl=0, dz=0, dd=0):
        return (wrap(lon + dl, n_lon), wrap(lat + dz, n_lat), wrap(dep + dd, n_depth))

    plane = [(i, d) for d in range(n_depth) for i in range(n_lon) if i or d]
    peers = [at(dl=i, dd=d) for i, d in plane] + [at(dz=z) for z in (1, -1)]
    peers += [at(dl=x, dz=z) for x in (1, -1) for z in (1, -1)]
    barrier = pltpu.get_barrier_semaphore()
    for peer in peers:
        pl.semaphore_signal(barrier, inc=1, device_id=peer, device_id_type=MESH)

    loads = [
        pltpu.make_async_copy(src, dst, in_sem.at[i])
        for i, (src, dst) in enumerate((
            (levels_in, st_lev), (ocean, st_ocean), (atlantic, st_atl), (mixing, st_mix),
            (direction, st_dir), (states, st_states),
        ))
    ]
    for load in loads:
        load.start()

    sends = []

    def send(src, dst, send_sem, recv_sem, device):
        copy = pltpu.make_async_remote_copy(
            src_ref=src, dst_ref=dst, send_sem=send_sem, recv_sem=recv_sem, device_id=device, device_id_type=MESH
        )
        copy.start()
        sends.append(copy)
        return copy

    upright = dep == 0
    own = lambda j: jnp.where(upright, j, layers - 1 - j)
    lane = lax.broadcasted_iota(jnp.int32, (rows, 128), 1)
    group = lane // HALO
    row = lax.broadcasted_iota(jnp.int32, (rows, 128), 0)

    width = jnp.zeros((rows, 128), jnp.float32)
    for r in range(rows):
        width = jnp.where(row == r, lat_width[r], width)
    square_row = lax.broadcasted_iota(jnp.int32, (rows, rows), 0)
    square_lane = lax.broadcasted_iota(jnp.int32, (rows, rows), 1)
    by_level = jnp.zeros((rows, 128), jnp.float32)
    for k in range(all_layers):
        line = cost_weight[pl.ds(jnp.where(upright, k, all_layers - 1 - k), 1), :]
        column = jnp.sum(jnp.where(square_row == square_lane, line, 0.0), axis=1, keepdims=True)
        by_level = jnp.where(lane == k, column * grid_scale, by_level)
    flat[0:rows, 0:128] = by_level
    dz_out[...] = jnp.zeros(dz_out.shape, jnp.float32) + level_dz[own(layers - 1)] * scale

    for load in loads:
        load.wait()
    basin = st_atl[...].astype(jnp.float32) * jnp.concatenate([width] * (columns // 128), axis=1)
    flat[0:rows, 128 : 128 + columns] = basin
    reach = st_lev[...] * st_ocean[...]

    edge = columns - 128
    packed = [[jnp.zeros((rows, 128), jnp.float32)] * 2 for _ in range(2)]

    def pack(pair, block, slot):
        right = pltpu.roll(block[:, edge:], (HALO * slot) % 128, 1)
        left = pltpu.roll(block[:, :128], (HALO * slot) % 128, 1)
        pair[0] = jnp.where(group == (slot - 1) % 32, right, pair[0])
        pair[1] = jnp.where(group == slot, left, pair[1])

    pack(packed[0], basin, 3 * layers)
    for j in range(layers):
        k = own(j)
        wet = dep * layers + k < reach
        couple = jnp.where(wet, math.sqrt(diffusion_step) * st_mix[k], 0.0)
        parts = [couple, st_dir[k]]
        parts += [jnp.where(wet, math.sqrt(3.0 * cubic_drag) * st_states[s, k], 0.0) for s in range(4)]
        for f, part in enumerate(parts):
            fields[f, j, 0:rows, 0:columns] = part
            pack(packed[f // 3], part, (f % 3) * layers + j)
    for m in range(2):
        for way in range(2):
            strips_out[m, way] = packed[m][way]

    pl.semaphore_wait(barrier, len(peers))

    arrivals = []
    near, far = slice(0, HALO), slice(rows - HALO, rows)
    below, above = slice(rows, rows + HALO), slice(rows + HALO, rows + 2 * HALO)

    def send_rows(ref, lead, lanes, first):
        a = send(ref.at[lead + (near, lanes)], ref.at[lead + (below, lanes)], lat_send.at[first], lat_recv.at[first], at(dz=-1))
        b = send(ref.at[lead + (far, lanes)], ref.at[lead + (above, lanes)], lat_send.at[first + 1], lat_recv.at[first + 1], at(dz=1))
        arrivals.extend((a, b))

    def send_strips(m):
        for way, dl in ((0, 1), (1, -1)):
            i = 2 * m + way
            arrivals.append(send(strips_out.at[m, way], strips_in.at[m, way, 0:rows], lon_send.at[i], lon_recv.at[i], at(dl=dl)))
            for up, (src, dst, dz) in enumerate(((near, below, -1), (far, above, 1))):
                i2 = 2 * i + up
                arrivals.append(send(strips_out.at[m, way, src], strips_in.at[m, way, dst], diag_send.at[i2], diag_recv.at[i2], at(dl=dl, dz=dz)))

    send_strips(0)
    send_rows(fields, (slice(0, 3), slice(0, layers)), slice(0, columns), 0)
    send_rows(flat, (), slice(0, 128 + columns), 2)
    send_strips(1)
    send_rows(fields, (slice(3, 6), slice(0, layers)), slice(0, columns), 4)
    dz_copy = send(dz_out, dz_in, dep_send.at[0], dep_recv.at[0], at(dd=1))
    for copy in arrivals:
        copy.wait_recv()

    lane_x = lax.broadcasted_iota(jnp.int32, (ext_rows, 128), 1)
    even = (lane_x // HALO) % 2 == 0

    def combine(pair):
        from_left, from_right = pair[0], pair[1]
        return [jnp.where(even, from_right, from_left), jnp.where(even, from_left, from_right)]

    def unpack(both, slot):
        return pltpu.roll(both[slot % 2], (128 - HALO * slot) % 128, 1)

    one = lambda flag: jnp.where(flag, 1.0, 0.0).astype(jnp.float32)
    lane_mask = jnp.where(lane_x < HALO, one(lon < n_lon - 1), jnp.where(lane_x >= 128 - HALO, one(lon > 0), 0.0))
    row_8 = lax.broadcasted_iota(jnp.int32, (2 * HALO, ext_columns), 0)
    row_mask = jnp.where(row_8 < HALO, one(lat < n_lat - 1), one(lat > 0))
    for m in range(2):
        both = combine(strips_in[m])
        for f in range(3):
            for j in range(layers):
                halo = unpack(both, f * layers + j)
                if m == 0 and f == 0:
                    halo = halo * lane_mask
                fields[3 * m + f, j, :, columns:] = halo
        if m == 0:
            flat[:, 128 + columns :] = unpack(both, 3 * layers)
    couple = fields.at[0]
    for j in range(layers):
        couple[j, rows:, :] = couple[j, rows:, :] * row_mask

    def send_level(ref, i):
        return send(ref.at[layers - 1], ref.at[layers], dep_send.at[i], dep_recv.at[i], at(dd=1))

    border = [send_level(fields.at[f], i) for f, i in ((0, 1), (1, 2), (5, 3))]

    tangents = [fields.at[1], tan1, tan2, tan3]
    drag = [fields.at[2 + s] for s in range(4)]

    def capacity_at(j):
        here = couple[j]
        total = around(here, couple[j - 1] if j else None, couple[j + 1])
        capacity[j] = jnp.where(here > 0.0, 1.0, 0.0) - here * total

    def tangent_at(s, j, out):
        value = tangents[s]
        damp = drag[s][j]
        return couple[j] * stencil(couple, value, j, layers) + (capacity[j] - damp * damp) * value[j]

    for j in range(layers - 1):
        capacity_at(j)
    for j in range(layers - 1):
        tan1[j] = tangent_at(0, j, None)
    for copy in border:
        copy.wait_recv()
    capacity_at(layers - 1)
    tan1[layers - 1] = tangent_at(0, layers - 1, None)
    pending = send_level(tan1, 4)

    def zonal(block, j):
        weighted = block[0:rows, 0:columns] * flat[0:rows, 128 : 128 + columns]
        folded = weighted[:, 0:128]
        for part in range(1, columns // 128):
            folded = folded + weighted[:, 128 * part : 128 * part + 128]
        return jnp.sum(folded, axis=1, keepdims=True) * (level_dz[own(j)] * scale)

    tiles = rows // 8
    lane_8 = lax.broadcasted_iota(jnp.int32, (8, 128), 1)
    sums = jnp.zeros((8, 128), jnp.float32)

    def put(sums, column, f, j):
        for t in range(tiles):
            slot = t * 2 * layers + f * layers + j
            sums = jnp.where(lane_8 == slot, column[8 * t : 8 * t + 8], sums)
        return sums

    last = drag[3]
    for j in range(layers):
        here = last[j]
        final = couple[j] * stencil(couple, last, j, layers) + (capacity[j] - here * here * (1.0 / 3.0)) * here
        sums = put(sums, zonal(final, j) * (1.0 / math.sqrt(3.0 * cubic_drag)), 0, j)

    for s in (1, 2):
        nxt = tangents[s + 1]
        for j in range(layers):
            if j == layers - 1:
                pending.wait_recv()
            nxt[j] = tangent_at(s, j, None)
        pending = send_level(nxt, 4 + s)

    pair = [jnp.zeros((rows, 128), jnp.float32)] * 2
    for j in range(layers):
        tan3_wide[j, 0:rows, 0:columns] = tan3[j, 0:rows, 0:columns]
        pack(pair, tan3[j, 0:rows, 0:columns], j)
    strip3_out[0] = pair[0]
    strip3_out[1] = pair[1]
    third = []
    for way, dl in ((0, 1), (1, -1)):
        third.append(send(strip3_out.at[way], strip3_in.at[way, 0:rows], t3_send.at[way], t3_recv.at[way], at(dl=dl)))
        for up, (src, dst, dz) in enumerate(((near, below, -1), (far, above, 1))):
            i = 2 + 2 * way + up
            third.append(send(strip3_out.at[way, src], strip3_in.at[way, dst], t3_send.at[i], t3_recv.at[i], at(dl=dl, dz=dz)))
    every = slice(0, layers)
    own_lanes = slice(0, columns)
    for i, (src, dst, dz) in enumerate(((near, below, -1), (far, above, 1))):
        third.append(send(tan3_wide.at[every, src, own_lanes], tan3_wide.at[every, dst, own_lanes], t3_send.at[6 + i], t3_recv.at[6 + i], at(dz=dz)))

    for j in range(layers):
        if j == layers - 1:
            pending.wait_recv()
        sums = put(sums, zonal(tangent_at(3, j, None), j), 1, j)

    zone[...] = sums
    zones[lon] = sums
    gathered = []
    for i, (dl, dd) in enumerate(plane):
        slot = lon + (n_lon if dd else 0)
        gathered.append(send(zone, zones.at[slot], zone_send.at[i], zone_recv.at[i], at(dl=dl, dd=dd)))

    for copy in third:
        copy.wait_recv()
    both = combine(strip3_in)
    for j in range(layers):
        tan3_wide[j, :, columns:] = unpack(both, j)
    for k in range(all_layers):
        weights[k] = jnp.broadcast_to(flat[:, k : k + 1], (ext_rows, 128))
    dz_copy.wait_recv()

    for copy in gathered:
        copy.wait_recv()
    mine = zones[0]
    other = zones[n_lon]
    for i in range(1, n_lon):
        mine = mine + zones[i]
        other = other + zones[n_lon + i]
    for t in range(tiles):
        shift = (128 - 2 * layers * t) % 128
        a = pltpu.roll(mine, shift, 1) if shift else mine
        b = pltpu.roll(other, (shift + 2 * layers) % 128, 1)
        totals[8 * t : 8 * t + 8] = jnp.where(lane_8 < 2 * layers, a, b)
    border = [
        send(totals.at[src], totals.at[dst], tot_send.at[i], tot_recv.at[i], at(dz=dz))
        for i, (src, dst, dz) in enumerate(((near, below, -1), (far, above, 1)))
    ]

    def place(f, k):
        if k < layers:
            return f * layers + k
        return 2 * layers + f * layers + (all_layers - 1 - k)

    def prefix_rows(part):
        count = part.stop - part.start
        streams = []
        for f in range(2):
            terms = [jnp.broadcast_to(totals[part, place(f, k) : place(f, k) + 1], (count, 128)) for k in range(all_layers)]
            stream = both_ways(terms, upright, False)
            if f == 0:
                streams = stream
            forced = [weights[k, part] * stream[k] for k in range(all_layers)]
            prefix = both_ways(forced, upright, True)
            for k in range(layers + 1):
                prefixes[f, k, part] = prefix[k]
        return streams

    streams = prefix_rows(slice(0, rows))
    spots = lax.broadcasted_iota(jnp.int32, (rows, rows), 0) == lax.broadcasted_iota(jnp.int32, (rows, rows), 1)
    for j in range(layers):
        line = jnp.sum(jnp.where(spots, streams[j][:, 0:rows], 0.0), axis=0, keepdims=True)
        overturning[pl.ds(own(j), 1), :] = line
    for copy in border:
        copy.wait_recv()
    prefix_rows(slice(rows, ext_rows))

    basin = flat[:, 128:]
    for j in range(layers + 1):
        if j < layers:
            area = basin * (level_dz[own(j)] * scale)
        else:
            area = basin * dz_in[0:1, 0:1]
        for f, ref in ((0, lam), (1, mu)):
            ref[0, j] = area * jnp.concatenate([prefixes[f, j]] * (ext_columns // 128), axis=1)

    ratio = 6.0 * cubic_drag / math.sqrt(3.0 * cubic_drag)
    pending = None
    for n, s in enumerate(reversed(range(4))):
        tangent = tan3_wide if s == 3 else tangents[s]
        for j in range(layers):
            if j == layers - 1 and pending is not None:
                for copy in pending:
                    copy.wait_recv()
            damp = drag[s][j]
            keep = capacity[j] - damp * damp
            here = lam[n, j]
            new_lam = couple[j] * stencil(couple, lam.at[n], j, layers) + keep * here
            new_mu = couple[j] * stencil(couple, mu.at[n], j, layers) + keep * mu[n, j]
            new_mu = new_mu - (ratio * damp) * (tangent[j] * here)
            if s:
                lam[n + 1, j] = new_lam
                mu[n + 1, j] = new_mu
            else:
                grad[own(j)] = new_lam[0:rows, 0:columns]
                hess[own(j)] = new_mu[0:rows, 0:columns]
        if s:
            pending = [send_level(lam.at[n + 1], 7 + 2 * n), send_level(mu.at[n + 1], 8 + 2 * n)]
    for copy in sends:
        copy.wait_send()


def both_ways(terms, upright, forward):
    count = len(terms)
    up = [terms[0]]
    for k in range(1, count):
        up.append(up[-1] + terms[k])
    down = [terms[-1]]
    for k in range(count - 2, -1, -1):
        down.append(down[-1] + terms[k])
    down = down[::-1]
    choose_up = upright if forward else jnp.logical_not(upright)
    return [jnp.where(choose_up, a, b) for a, b in zip(up, down)]


def solution(mesh):
    n_lon, n_lat, n_depth = (mesh.shape[name] for name in ("lon", "lat", "depth"))

    def shards(states, direction, mixing, level_dz, lat_width, cost_weight, ocean_columns, atlantic, levels):
        layers, rows, columns = direction.shape
        ext = (rows + 2 * HALO, columns + 128)
        tall = (layers + 1,) + ext
        f32, i32 = jnp.float32, jnp.int32
        vmem = lambda *shape: pltpu.VMEM(shape, f32)
        dma = lambda count: pltpu.SemaphoreType.DMA((count,))
        in_vmem, in_smem, anywhere = (pl.BlockSpec(memory_space=m) for m in (pltpu.VMEM, pltpu.SMEM, pl.ANY))
        scale = 1.0 / math.sqrt(columns * n_lon * layers * n_depth)
        body = functools.partial(kernel, n_lon, n_lat, n_depth, scale, math.sqrt(columns * n_lon))
        return pl.pallas_call(
            body,
            out_shape=(
                jax.ShapeDtypeStruct(direction.shape, f32),
                jax.ShapeDtypeStruct(direction.shape, f32),
                jax.ShapeDtypeStruct((layers, rows), f32),
            ),
            in_specs=[anywhere] * 3 + [in_smem] * 2 + [in_vmem] + [anywhere] * 3,
            out_specs=(in_vmem,) * 3,
            scratch_shapes=[
                vmem(*states.shape), vmem(*direction.shape), vmem(*direction.shape),
                pltpu.VMEM((rows, columns), i32), pltpu.VMEM((rows, columns), i32), pltpu.VMEM((rows, columns), i32),
                vmem(6, *tall), vmem(layers, *ext), vmem(*tall), vmem(*tall), vmem(*tall), vmem(8, 128),
                vmem(layers, *ext), vmem(4, *tall), vmem(4, *tall),
                vmem(ext[0], 128 + ext[1]), vmem(2, 2, rows, 128), vmem(2, 2, ext[0], 128),
                vmem(2, rows, 128), vmem(2, ext[0], 128), vmem(8, 128), vmem(8, 128),
                vmem(8, 128), vmem(2 * n_lon, 8, 128), vmem(ext[0], 128),
                vmem(2, layers + 1, ext[0], 128), vmem(n_depth * layers, ext[0], 128),
                dma(6), dma(6), dma(6), dma(4), dma(4), dma(8), dma(8), dma(16), dma(16),
                dma(2 * n_lon - 1), dma(2 * n_lon - 1), dma(2), dma(2), dma(8), dma(8),
            ],
            compiler_params=pltpu.CompilerParams(
                collective_id=0, has_side_effects=True, vmem_limit_bytes=48 * 2**20
            ),
            cost_estimate=pl.CostEstimate(flops=3 * 10**7, bytes_accessed=3 * 10**6, transcendentals=0),
        )(states, direction, mixing, level_dz, lat_width, cost_weight, ocean_columns, atlantic, levels)

    placed = (
        P(None, "depth", "lat", "lon"),
        P("depth", "lat", "lon"),
        P("depth", "lat", "lon"),
        P("depth"),
        P("lat"),
        P(None, "lat"),
        P("lat", "lon"),
        P("lat", "lon"),
        P("lat", "lon"),
    )
    return jax.shard_map(
        shards,
        mesh=mesh,
        in_specs=placed,
        out_specs=(P("depth", "lat", "lon"), P("depth", "lat", "lon"), P("depth", "lat")),
        check_vma=False,
    )
```

```python
import functools
import math

import jax
import jax.numpy as jnp
from jax import lax
from jax.experimental import pallas as pl
from jax.experimental.pallas import tpu as pltpu
from jax.sharding import PartitionSpec as P

MESH = pl.DeviceIdType.MESH
diffusion_step = 0.08
cubic_drag = 0.15

HALO = 4
LINE = 4


def around(couple, value, level, part, here=None):
    if here is None:
        here = couple[level] if value is None else couple[level] * value[level]
    rows, columns = here.shape
    total = pltpu.roll(here, 1, 1) + pltpu.roll(here, columns - 1, 1)
    total = (total + (pltpu.roll(here, 1, 0) + pltpu.roll(here, rows - 1, 0)))[part]
    for k in (level - 1, level + 1):
        if k >= 0:
            there = couple[(k,) + part]
            total = total + (there if value is None else there * value[(k,) + part])
    return total


def kernel(
    n_lon, n_lat, n_depth, scale, grid_scale,
    states, direction, mixing, dz_in_hbm, width_in_hbm, weight_in_hbm, ocean, atlantic, levels_in,
    hess, grad, overturning,
    st_states, st_dir, st_mix, st_ocean, st_atl, st_lev, cost_weight, level_dz, lat_width,
    fields, capacity, tan1, tan2, tan3, tan3_wide, lam, mu,
    flat, edges, rows_out, rows_in, strips_out, strips_in, strip3_out, strip3_in, dz_out, dz_in, zone, zones, totals, prefixes, weights,
    in_sem, lat_send, lat_recv, lon_send, lon_recv, dep_send, dep_recv, zone_send, zone_recv, ready,
):
    layers, rows, columns = direction.shape
    all_layers = 2 * layers
    ext_rows, ext_columns = fields.shape[-2:]
    lon, lat, dep = lax.axis_index("lon"), lax.axis_index("lat"), lax.axis_index("depth")
    wrap = lambda value, size: lax.rem(value + size, size)

    def at(dl=0, dz=0, dd=0):
        return (wrap(lon + dl, n_lon), wrap(lat + dz, n_lat), wrap(dep + dd, n_depth))

    plane = [(i, d) for d in range(n_depth) for i in range(n_lon) if i or d]
    start = lon // LINE * LINE
    across = [at(dl=LINE * i) for i in range(1, n_lon // LINE)]
    peers = [
        (start + lax.rem(lon - start + i, LINE), lat, wrap(dep + d, n_depth))
        for d in range(n_depth) for i in range(LINE) if i or d
    ]
    peers += across + [at(dl=i) for i in (1, -1)] + [at(dz=z) for z in (1, -1)]
    barrier = pltpu.get_barrier_semaphore()
    for peer in peers:
        pl.semaphore_signal(barrier, inc=1, device_id=peer, device_id_type=MESH)

    loads = [
        pltpu.make_async_copy(src, dst, in_sem.at[i])
        for i, (src, dst) in enumerate((
            (width_in_hbm, lat_width), (weight_in_hbm, cost_weight), (dz_in_hbm, level_dz), (levels_in, st_lev),
            (ocean, st_ocean), (atlantic, st_atl), (mixing, st_mix), (direction, st_dir), (states, st_states),
        ))
    ]
    for load in loads:
        load.start()

    sends, expected = [], {}

    def send(src, dst, send_sem, recv_sem, device):
        copy = pltpu.make_async_remote_copy(
            src_ref=src, dst_ref=dst, send_sem=send_sem, recv_sem=recv_sem, device_id=device, device_id_type=MESH
        )
        copy.start()
        sends.append(copy)
        expected[id(copy)] = copy
        return copy

    def arrive(*copies):
        for copy in copies:
            expected.pop(id(copy)).wait_recv()

    def finish():
        for copy in list(expected.values()):
            arrive(copy)
        for copy in sends:
            copy.wait_send()

    upright = dep == 0
    own = lambda j: jnp.where(upright, j, layers - 1 - j)
    lane = lax.broadcasted_iota(jnp.int32, (rows, 128), 1)
    group = lane // HALO
    row = lax.broadcasted_iota(jnp.int32, (rows, 128), 0)

    for load in loads[:3]:
        load.wait()
    width = jnp.zeros((rows, 128), jnp.float32)
    for r in range(rows):
        width = jnp.where(row == r, lat_width[r], width)
    square_row = lax.broadcasted_iota(jnp.int32, (rows, rows), 0)
    square_lane = lax.broadcasted_iota(jnp.int32, (rows, rows), 1)
    by_level = jnp.zeros((rows, 128), jnp.float32)
    for k in range(all_layers):
        line = cost_weight[pl.ds(jnp.where(upright, k, all_layers - 1 - k), 1), :]
        column = jnp.sum(jnp.where(square_row == square_lane, line, 0.0), axis=1, keepdims=True)
        by_level = jnp.where(lane == k, column * grid_scale, by_level)
    flat[0:rows, 0:128] = by_level
    dz_out[...] = jnp.zeros(dz_out.shape, jnp.float32) + level_dz[own(layers - 1)] * scale

    for load in loads[3:]:
        load.wait()
    basin = st_atl[...].astype(jnp.float32) * jnp.concatenate([width] * (columns // 128), axis=1)
    flat[0:rows, 128 : 128 + columns] = basin
    reach = st_lev[...] * st_ocean[...]

    edge = columns - 128
    packed = [[jnp.zeros((rows, 128), jnp.float32)] * 2 for _ in range(2)]

    def pack(pair, block, slot):
        right = pltpu.roll(block[:, edge:], (HALO * slot) % 128, 1)
        left = pltpu.roll(block[:, :128], (HALO * slot) % 128, 1)
        pair[0] = jnp.where(group == (slot - 1) % 32, right, pair[0])
        pair[1] = jnp.where(group == slot, left, pair[1])

    pack(packed[0], basin, 3 * layers)
    upper = lax.broadcasted_iota(jnp.int32, (2 * HALO, columns), 0) < HALO
    held = None
    for j in range(layers):
        k = own(j)
        wet = dep * layers + k < reach
        couple = jnp.where(wet, math.sqrt(diffusion_step) * st_mix[k], 0.0)
        parts = [couple, st_dir[k]]
        parts += [jnp.where(wet, math.sqrt(3.0 * cubic_drag) * st_states[s, k], 0.0) for s in range(4)]
        for f, part in enumerate(parts):
            fields[f, j, 0:rows, 0:columns] = part
            pack(packed[f // 3], part, (f % 3) * layers + j)
            if f < 3 and j % 2:
                before, after = held[f][0 : 2 * HALO], pltpu.roll(part[0 : 2 * HALO], HALO, 0)
                rows_out[0, f, j // 2] = jnp.where(upper, before, after)
                before, after = held[f][rows - 2 * HALO :], pltpu.roll(part[rows - 2 * HALO :], HALO, 0)
                rows_out[1, f, j // 2] = jnp.where(upper, after, before)
        held = parts
    for m in range(2):
        for way in range(2):
            strips_out[m, way] = packed[m][way]

    pl.semaphore_wait(barrier, len(peers))
    for peer in across:
        pl.semaphore_signal(ready, inc=1, device_id=peer, device_id_type=MESH)

    every = slice(0, layers)
    inner = (slice(0, rows), slice(0, columns))
    bottom = (slice(rows, ext_rows), slice(0, ext_columns))
    side = (slice(0, rows), slice(columns, ext_columns))
    frame = (bottom, side)
    whole = (slice(0, ext_rows), slice(0, ext_columns))
    bottom_level = layers - 1

    def send_rows(ref, lead, lanes, i, first=0, last=HALO):
        near, below = slice(first, last), slice(rows + first, rows + last)
        far, above = slice(rows - last, rows - first), slice(ext_rows - last, ext_rows - first)
        return [
            send(ref.at[lead + (src, lanes)], ref.at[lead + (dst, lanes)], lat_send.at[2 * i + n], lat_recv.at[2 * i + n], at(dz=dz))
            for n, (src, dst, dz) in enumerate(((near, below, -1), (far, above, 1)))
        ]

    def send_strips(out, into, i):
        return [
            send(out.at[way], into.at[way, 0:rows], lon_send.at[2 * i + way], lon_recv.at[2 * i + way], at(dl=dl))
            for way, dl in ((0, 1), (1, -1))
        ]

    def send_part(src, dst, i):
        return send(src, dst, dep_send.at[i], dep_recv.at[i], at(dd=1))

    def send_level(ref, i):
        return send_part(ref.at[bottom_level], ref.at[layers], i)

    strips = send_strips(strips_out.at[0], strips_in.at[0], 0)
    first_rows = [
        send(rows_out.at[i], rows_in.at[i], lat_send.at[i], lat_recv.at[i], at(dz=dz)) for i, dz in ((0, -1), (1, 1))
    ]
    strips += send_strips(strips_out.at[1], strips_in.at[1], 1)
    last_rows = [
        send(
            fields.at[5, every, pl.ds(src, 1), inner[1]], edges.at[every, pl.ds(dst, 1), inner[1]],
            lat_send.at[2 + i], lat_recv.at[2 + i], at(dz=dz),
        )
        for i, (src, dst, dz) in enumerate(((0, 0, -1), (rows - 1, 2 * HALO - 1, 1)))
    ]
    first_level = [
        send_part(fields.at[(slice(0, 2), bottom_level) + inner], fields.at[(slice(0, 2), layers) + inner], 0),
        send_part(fields.at[(5, bottom_level) + inner], fields.at[(5, layers) + inner], 1),
        send_part(dz_out, dz_in, 2),
    ]

    arrive(*strips)
    corners = send_rows(strips_in, (slice(0, 2), slice(0, 2)), slice(0, 128), 2)
    drag_rows = [
        send_rows(fields, (3, every), inner[1], 3, 0, 2),
        send_rows(fields, (4, every), inner[1], 4, 0, 2),
    ]
    flat_rows = send_rows(flat, (), slice(0, 128 + columns), 6)

    lane_x = lax.broadcasted_iota(jnp.int32, (ext_rows, 128), 1)
    even = (lane_x // HALO) % 2 == 0

    def combine(pair, part):
        from_left, from_right = pair[0, part], pair[1, part]
        return [jnp.where(even[part], from_right, from_left), jnp.where(even[part], from_left, from_right)]

    def unpack(both, slot):
        return pltpu.roll(both[slot % 2], (128 - HALO * slot) % 128, 1)

    one = lambda flag: jnp.where(flag, 1.0, 0.0).astype(jnp.float32)
    lane_mask = jnp.where(lane_x < HALO, one(lon < n_lon - 1), jnp.where(lane_x >= 128 - HALO, one(lon > 0), 0.0))
    row_8 = lax.broadcasted_iota(jnp.int32, (2 * HALO, ext_columns), 0)
    row_mask = jnp.where(row_8 < HALO, one(lat < n_lat - 1), one(lat > 0))
    couple = fields.at[0]

    def unpack_all(part):
        for m in range(2):
            both = combine(strips_in.at[m], part)
            for f in range(3):
                for j in range(layers):
                    halo = unpack(both, f * layers + j)
                    if m == 0 and f == 0:
                        halo = halo * lane_mask[part]
                        if part.start:
                            halo = halo * row_mask[:, columns:]
                    fields[3 * m + f, j, part, columns:] = halo
            if m == 0:
                flat[part, 128 + columns :] = unpack(both, 3 * layers)

    unpack_all(slice(0, rows))
    arrive(*first_rows)
    for f in range(3):
        for pair in range(layers // 2):
            from_next, from_previous = rows_in[0, f, pair], rows_in[1, f, pair]
            both = [
                jnp.where(upper, from_next, from_previous),
                pltpu.roll(jnp.where(upper, from_previous, from_next), HALO, 0),
            ]
            for odd in range(2):
                halo = both[odd] if f else both[odd] * row_mask[:, 0:columns]
                fields[f, 2 * pair + odd, rows:, 0:columns] = halo
    arrive(*last_rows)
    arrive(*first_level)

    tangents = [fields.at[1], tan1, tan2, tan3]
    drag = [fields.at[2 + s] for s in range(4)]

    def capacity_at(j, part):
        here = couple[(j,) + part]
        capacity[(j,) + part] = jnp.where(here > 0.0, 1.0, 0.0) - here * around(couple, None, j, part)

    def tangent_at(s, j, part):
        value = tangents[s]
        at_part = (j,) + part
        damp = drag[s][at_part]
        return couple[at_part] * around(couple, value, j, part) + (capacity[at_part] - damp * damp) * value[at_part]

    def zonal(block, j):
        weighted = block * flat[0:rows, 128 : 128 + columns]
        folded = weighted[:, 0:128]
        for part in range(1, columns // 128):
            folded = folded + weighted[:, 128 * part : 128 * part + 128]
        return jnp.sum(folded, axis=1, keepdims=True) * (level_dz[own(j)] * scale)

    tiles = rows // 8
    lane_8 = lax.broadcasted_iota(jnp.int32, (8, 128), 1)

    def put(sums, column, j):
        for t in range(tiles):
            sums = jnp.where(lane_8 == t * layers + j, column[8 * t : 8 * t + 8], sums)
        return sums

    def gather(f, sums):
        zone[f] = sums
        zones[f, lon] = sums
        return [
            send(zone.at[f], zones.at[f, lon + (n_lon if dd else 0)], zone_send.at[f, i], zone_recv.at[f, i], at(dl=dl, dd=dd))
            for i, (dl, dd) in enumerate(plane)
        ]

    last = drag[3]
    sums = jnp.zeros((8, 128), jnp.float32)
    for j in range(layers):
        capacity_at(j, inner)
    for j in range(layers):
        here = last[(j,) + inner]
        outer = jnp.concatenate([edges[j], jnp.zeros((2 * HALO, ext_columns - columns), jnp.float32)], axis=1)
        spread = jnp.concatenate([couple[j, 0:rows] * last[j, 0:rows], couple[j, rows:] * outer], axis=0)
        final = couple[(j,) + inner] * around(couple, last, j, inner, spread)
        final = final + (capacity[(j,) + inner] - here * here * (1.0 / 3.0)) * here
        sums = put(sums, zonal(final, j) * (1.0 / math.sqrt(3.0 * cubic_drag)), j)
    pl.semaphore_wait(ready, len(across))
    gathered_0 = gather(0, sums)
    drag_rows.append(send_rows(fields, (5, every), inner[1], 5, 0, 3))
    for j in range(layers):
        tan1[(j,) + inner] = tangent_at(0, j, inner)

    arrive(*corners)
    unpack_all(slice(rows, ext_rows))
    border = [
        send_part(fields.at[(slice(0, 2), bottom_level) + part], fields.at[(slice(0, 2), layers) + part], 3 + i)
        for i, part in enumerate(frame)
    ]
    for j in range(layers):
        if j == bottom_level:
            arrive(*border)
        for part in frame:
            capacity_at(j, part)
            tan1[(j,) + part] = tangent_at(0, j, part)
    pending = send_level(tan1, 5)

    for s in (1, 2):
        nxt = tangents[s + 1]
        arrive(*drag_rows[s - 1])
        for j in range(layers):
            if j == bottom_level:
                arrive(pending)
            nxt[j] = tangent_at(s, j, whole)
        pending = send_level(nxt, 5 + s)

    pair = [jnp.zeros((rows, 128), jnp.float32)] * 2
    for j in range(layers):
        block = tan3[(j,) + inner]
        tan3_wide[(j,) + inner] = block
        pack(pair, block, j)
    strip3_out[0] = pair[0]
    strip3_out[1] = pair[1]
    strips = send_strips(strip3_out, strip3_in, 2)
    third_rows = send_rows(tan3_wide, (every,), inner[1], 7)

    sums = jnp.zeros((8, 128), jnp.float32)
    for j in range(layers):
        if j == bottom_level:
            arrive(pending)
        sums = put(sums, zonal(tangent_at(3, j, inner), j), j)
    gathered_1 = gather(1, sums)

    def collect(f):
        mine = zones[f, 0]
        other = zones[f, n_lon]
        for i in range(1, n_lon):
            mine = mine + zones[f, i]
            other = other + zones[f, n_lon + i]
        for t in range(tiles):
            shift = (128 - layers * t) % 128
            a = pltpu.roll(mine, shift, 1) if shift else mine
            b = pltpu.roll(other, (shift + layers) % 128, 1)
            totals[f, 8 * t : 8 * t + 8] = jnp.where(lane_8 < layers, a, b)
        return send_rows(totals, (f,), slice(0, 128), 8 + f)

    def prefix_rows(f, part):
        count = part.stop - part.start
        places = [k if k < layers else layers + all_layers - 1 - k for k in range(all_layers)]
        terms = [jnp.broadcast_to(totals[f, part, p : p + 1], (count, 128)) for p in places]
        stream = both_ways(terms, upright, False)
        prefix = both_ways([weights[k, part] * stream[k] for k in range(all_layers)], upright, True)
        for k in range(layers + 1):
            prefixes[f, k, part] = prefix[k]
        return stream

    arrive(*flat_rows, *drag_rows[2])
    for k in range(all_layers):
        weights[k] = jnp.broadcast_to(flat[:, k : k + 1], (ext_rows, 128))

    def start_adjoint(f, ref):
        basin = flat[:, 128:]
        for j in range(layers + 1):
            thick = level_dz[own(j)] * scale if j < layers else dz_in[0:1, 0:1]
            ref[0, j] = basin * thick * jnp.concatenate([prefixes[f, j]] * (ext_columns // 128), axis=1)

    def adjoint_at(ref, n, j, part):
        at_part = (j,) + part
        damp = drag[3 - n][at_part]
        keep = capacity[at_part] - damp * damp
        return couple[at_part] * around(couple, ref.at[n], j, part) + keep * ref[(n,) + at_part], damp

    def lam_step(n, waits):
        for j in range(layers):
            if j == bottom_level:
                arrive(*waits)
            if n < 3:
                lam[n + 1, j] = adjoint_at(lam, n, j, whole)[0]
            else:
                grad[own(j)] = adjoint_at(lam, n, j, inner)[0]
        return [send_level(lam.at[n + 1], 8 + n)] if n < 3 else []

    ratio = 6.0 * cubic_drag / math.sqrt(3.0 * cubic_drag)

    def mu_step(n, waits):
        part = whole if n < 3 else inner
        tangent = tan3_wide if n == 0 else tangents[3 - n]
        for j in range(layers):
            if j == bottom_level:
                arrive(*waits)
            new, damp = adjoint_at(mu, n, j, part)
            new = new - (ratio * damp) * (tangent[(j,) + part] * lam[(n, j) + part])
            if n < 3:
                mu[n + 1, j] = new
            else:
                hess[own(j)] = new
        return [send_level(mu.at[n + 1], 11 + n)] if n < 3 else []

    arrive(*gathered_0)
    border = collect(0)
    streams = prefix_rows(0, slice(0, rows))
    spots = lax.broadcasted_iota(jnp.int32, (rows, rows), 0) == lax.broadcasted_iota(jnp.int32, (rows, rows), 1)
    for j in range(layers):
        line = jnp.sum(jnp.where(spots, streams[j][:, 0:rows], 0.0), axis=0, keepdims=True)
        overturning[pl.ds(own(j), 1), :] = line
    arrive(*strips)
    corners = send_rows(strip3_in, (slice(0, 2),), slice(0, 128), 10)
    arrive(*border)
    prefix_rows(0, slice(rows, ext_rows))
    start_adjoint(0, lam)
    pending = lam_step(0, [])
    pending = lam_step(1, pending)

    arrive(*gathered_1)
    border = collect(1)
    prefix_rows(1, slice(0, rows))
    arrive(*third_rows, *corners)
    both = combine(strip3_in, slice(0, ext_rows))
    for j in range(layers):
        tan3_wide[j, :, columns:] = unpack(both, j)
    pending = lam_step(2, pending)
    lam_step(3, pending)

    arrive(*border)
    prefix_rows(1, slice(rows, ext_rows))
    start_adjoint(1, mu)
    pending = []
    for n in range(4):
        pending = mu_step(n, pending)
    finish()


def both_ways(terms, upright, forward):
    count = len(terms)
    up = [terms[0]]
    for k in range(1, count):
        up.append(up[-1] + terms[k])
    down = [terms[-1]]
    for k in range(count - 2, -1, -1):
        down.append(down[-1] + terms[k])
    down = down[::-1]
    choose_up = upright if forward else jnp.logical_not(upright)
    return [jnp.where(choose_up, a, b) for a, b in zip(up, down)]


def store(hess, grad, overturning, hess_out, grad_out, overturning_out, sem):
    copies = [
        pltpu.make_async_copy(src, dst, sem.at[i])
        for i, (src, dst) in enumerate(((hess, hess_out), (grad, grad_out), (overturning, overturning_out)))
    ]
    for copy in copies:
        copy.start()
    for copy in copies:
        copy.wait()


def solution(mesh):
    n_lon, n_lat, n_depth = (mesh.shape[name] for name in ("lon", "lat", "depth"))

    def shards(states, direction, mixing, level_dz, lat_width, cost_weight, ocean_columns, atlantic, levels):
        layers, rows, columns = direction.shape
        ext = (rows + 2 * HALO, columns + 128)
        tall = (layers + 1,) + ext
        f32, i32 = jnp.float32, jnp.int32
        vmem = lambda *shape: pltpu.VMEM(shape, f32)
        dma = lambda count: pltpu.SemaphoreType.DMA((count,))
        in_vmem, in_hbm = (pl.BlockSpec(memory_space=m) for m in (pltpu.VMEM, pltpu.HBM))
        scale = 1.0 / math.sqrt(columns * n_lon * layers * n_depth)
        body = functools.partial(kernel, n_lon, n_lat, n_depth, scale, math.sqrt(columns * n_lon))
        results = pl.pallas_call(
            body,
            out_shape=(vmem(*direction.shape), vmem(*direction.shape), vmem(layers, rows)),
            in_specs=[in_hbm] * 9,
            out_specs=(in_vmem,) * 3,
            scratch_shapes=[
                vmem(*states.shape), vmem(*direction.shape), vmem(*direction.shape),
                pltpu.VMEM((rows, columns), i32), pltpu.VMEM((rows, columns), i32), pltpu.VMEM((rows, columns), i32),
                vmem(*cost_weight.shape), pltpu.SMEM(level_dz.shape, f32), pltpu.SMEM(lat_width.shape, f32),
                vmem(6, *tall), vmem(layers, *ext), vmem(*tall), vmem(*tall), vmem(*tall),
                vmem(layers, *ext), vmem(4, *tall), vmem(4, *tall),
                vmem(ext[0], 128 + ext[1]), vmem(layers, 2 * HALO, columns),
                vmem(2, 3, layers // 2, 2 * HALO, columns), vmem(2, 3, layers // 2, 2 * HALO, columns),
                vmem(2, 2, rows, 128), vmem(2, 2, ext[0], 128),
                vmem(2, rows, 128), vmem(2, ext[0], 128), vmem(8, 128), vmem(8, 128),
                vmem(2, 8, 128), vmem(2, 2 * n_lon, 8, 128), vmem(2, ext[0], 128),
                vmem(2, layers + 1, ext[0], 128), vmem(n_depth * layers, ext[0], 128),
                dma(9), dma(22), dma(22), dma(6), dma(6), dma(14), dma(14),
                pltpu.SemaphoreType.DMA((2, 2 * n_lon - 1)), pltpu.SemaphoreType.DMA((2, 2 * n_lon - 1)),
                pltpu.SemaphoreType.REGULAR,
            ],
            compiler_params=pltpu.CompilerParams(
                collective_id=0, has_side_effects=True, vmem_limit_bytes=48 * 2**20
            ),
            cost_estimate=pl.CostEstimate(flops=3 * 10**7, bytes_accessed=3 * 10**6, transcendentals=0),
        )(*(
            pltpu.with_memory_space_constraint(x, pltpu.HBM)
            for x in (states, direction, mixing, level_dz, lat_width, cost_weight, ocean_columns, atlantic, levels)
        ))
        return pl.pallas_call(
            store,
            out_shape=tuple(jax.ShapeDtypeStruct(result.shape, f32) for result in results),
            in_specs=[in_vmem] * 3,
            out_specs=(in_hbm,) * 3,
            scratch_shapes=[dma(3)],
            cost_estimate=pl.CostEstimate(flops=0, bytes_accessed=10**6, transcendentals=0),
        )(*(pltpu.with_memory_space_constraint(result, pltpu.VMEM) for result in results))

    placed = (
        P(None, "depth", "lat", "lon"),
        P("depth", "lat", "lon"),
        P("depth", "lat", "lon"),
        P("depth"),
        P("lat"),
        P(None, "lat"),
        P("lat", "lon"),
        P("lat", "lon"),
        P("lat", "lon"),
    )
    return jax.shard_map(
        shards,
        mesh=mesh,
        in_specs=placed,
        out_specs=(P("depth", "lat", "lon"), P("depth", "lat", "lon"), P("depth", "lat")),
        check_vma=False,
    )
```

```python
import functools
import itertools
import math

import jax
import jax.numpy as jnp
from jax import lax
from jax.experimental import pallas as pl
from jax.experimental.pallas import tpu as pltpu
from jax.sharding import PartitionSpec as P

MESH = pl.DeviceIdType.MESH
diffusion_step = 0.08
cubic_drag = 0.15

HALO = 4
LINE = 4
DEEP = 4


def around(couple, value, level, part, here=None):
    if here is None:
        here = couple[level] if value is None else couple[level] * value[level]
    rows, columns = here.shape
    total = pltpu.roll(here, 1, 1) + pltpu.roll(here, columns - 1, 1)
    total = (total + (pltpu.roll(here, 1, 0) + pltpu.roll(here, rows - 1, 0)))[part]
    for k in (level - 1, level + 1):
        if k >= 0:
            there = couple[(k,) + part]
            total = total + (there if value is None else there * value[(k,) + part])
    return total


def kernel(
    n_lon, n_lat, n_depth, scale, grid_scale,
    states, direction, mixing, dz_in_hbm, width_in_hbm, weight_in_hbm, ocean, atlantic, levels_in,
    hess, grad, overturning,
    st_states, st_dir, st_mix, st_ocean, st_atl, st_lev, cost_weight, level_dz, lat_width,
    fields, capacity, tan1, tan2, tan3, tan3_wide, lam, mu,
    flat, edges, rows_out, rows_in, strips_out, strips_in, strip3_out, strip3_in, dz_out, dz_in, zone, zones, totals, prefixes, weights,
    in_sem, lat_send, lat_recv, lon_send, lon_recv, dep_send, dep_recv, zone_send, zone_recv, ready,
):
    layers, rows, columns = direction.shape
    all_layers = 2 * layers
    ext_rows, ext_columns = fields.shape[-2:]
    lon, lat, dep = lax.axis_index("lon"), lax.axis_index("lat"), lax.axis_index("depth")
    wrap = lambda value, size: lax.rem(value + size, size)

    def at(dl=0, dz=0, dd=0):
        return (wrap(lon + dl, n_lon), wrap(lat + dz, n_lat), wrap(dep + dd, n_depth))

    plane = [(i, d) for d in range(n_depth) for i in range(n_lon) if i or d]
    start = lon // LINE * LINE
    across = [at(dl=LINE * i) for i in range(1, n_lon // LINE)]
    peers = [
        (start + lax.rem(lon - start + i, LINE), lat, wrap(dep + d, n_depth))
        for d in range(n_depth) for i in range(LINE) if i or d
    ]
    peers += across + [at(dl=i) for i in (1, -1)] + [at(dz=z) for z in (1, -1)]
    barrier = pltpu.get_barrier_semaphore()
    for peer in peers:
        pl.semaphore_signal(barrier, inc=1, device_id=peer, device_id_type=MESH)

    loads = [
        pltpu.make_async_copy(src, dst, in_sem.at[i])
        for i, (src, dst) in enumerate((
            (width_in_hbm, lat_width), (weight_in_hbm, cost_weight), (dz_in_hbm, level_dz), (levels_in, st_lev),
            (ocean, st_ocean), (atlantic, st_atl), (mixing, st_mix), (direction, st_dir), (states, st_states),
        ))
    ]
    for load in loads:
        load.start()

    sends, expected = [], {}

    def send(src, dst, send_sem, recv_sem, device):
        copy = pltpu.make_async_remote_copy(
            src_ref=src, dst_ref=dst, send_sem=send_sem, recv_sem=recv_sem, device_id=device, device_id_type=MESH
        )
        copy.start()
        sends.append(copy)
        expected[id(copy)] = copy
        return copy

    def arrive(*copies):
        for copy in copies:
            expected.pop(id(copy)).wait_recv()

    def finish():
        for copy in list(expected.values()):
            arrive(copy)
        for copy in sends:
            copy.wait_send()

    upright = dep == 0
    own = lambda j: jnp.where(upright, j, layers - 1 - j)
    lane = lax.broadcasted_iota(jnp.int32, (rows, 128), 1)
    group = lane // HALO
    row = lax.broadcasted_iota(jnp.int32, (rows, 128), 0)

    for load in loads[:3]:
        load.wait()
    width = jnp.zeros((rows, 128), jnp.float32)
    for r in range(rows):
        width = jnp.where(row == r, lat_width[r], width)
    square_row = lax.broadcasted_iota(jnp.int32, (rows, rows), 0)
    square_lane = lax.broadcasted_iota(jnp.int32, (rows, rows), 1)
    by_level = jnp.zeros((rows, 128), jnp.float32)
    for k in range(all_layers):
        line = cost_weight[pl.ds(jnp.where(upright, k, all_layers - 1 - k), 1), :]
        column = jnp.sum(jnp.where(square_row == square_lane, line, 0.0), axis=1, keepdims=True)
        by_level = jnp.where(lane == k, column * grid_scale, by_level)
    flat[0:rows, 0:128] = by_level
    thick = jnp.zeros(dz_out.shape, jnp.float32)
    for i in range(DEEP):
        thick = jnp.where(lax.broadcasted_iota(jnp.int32, dz_out.shape, 0) == i, level_dz[own(layers - 1 - i)] * scale, thick)
    dz_out[...] = thick

    for load in loads[3:]:
        load.wait()
    basin = st_atl[...].astype(jnp.float32) * jnp.concatenate([width] * (columns // 128), axis=1)
    flat[0:rows, 128 : 128 + columns] = basin
    reach = st_lev[...] * st_ocean[...]

    edge = columns - 128
    packed = [[jnp.zeros((rows, 128), jnp.float32)] * 2 for _ in range(2)]

    def pack(pair, block, slot):
        right = pltpu.roll(block[:, edge:], (HALO * slot) % 128, 1)
        left = pltpu.roll(block[:, :128], (HALO * slot) % 128, 1)
        pair[0] = jnp.where(group == (slot - 1) % 32, right, pair[0])
        pair[1] = jnp.where(group == slot, left, pair[1])

    pack(packed[0], basin, 3 * layers)
    upper = lax.broadcasted_iota(jnp.int32, (2 * HALO, columns), 0) < HALO
    held = None
    for j in range(layers):
        k = own(j)
        wet = dep * layers + k < reach
        couple = jnp.where(wet, math.sqrt(diffusion_step) * st_mix[k], 0.0)
        parts = [couple, st_dir[k]]
        parts += [jnp.where(wet, math.sqrt(3.0 * cubic_drag) * st_states[s, k], 0.0) for s in range(4)]
        for f, part in enumerate(parts):
            fields[f, j, 0:rows, 0:columns] = part
            pack(packed[f // 3], part, (f % 3) * layers + j)
            if f < 3 and j % 2:
                before, after = held[f][0 : 2 * HALO], pltpu.roll(part[0 : 2 * HALO], HALO, 0)
                rows_out[0, f, j // 2] = jnp.where(upper, before, after)
                before, after = held[f][rows - 2 * HALO :], pltpu.roll(part[rows - 2 * HALO :], HALO, 0)
                rows_out[1, f, j // 2] = jnp.where(upper, after, before)
        held = parts
    for m in range(2):
        for way in range(2):
            strips_out[m, way] = packed[m][way]

    pl.semaphore_wait(barrier, len(peers))
    for peer in across:
        pl.semaphore_signal(ready, inc=1, device_id=peer, device_id_type=MESH)

    every = slice(0, layers)
    inner = (slice(0, rows), slice(0, columns))
    bottom = (slice(rows, ext_rows), slice(0, ext_columns))
    side = (slice(0, rows), slice(columns, ext_columns))
    frame = (bottom, side)
    whole = (slice(0, ext_rows), slice(0, ext_columns))
    bottom_level = layers - 1

    def send_rows(ref, lead, lanes, i, first=0, last=HALO):
        near, below = slice(first, last), slice(rows + first, rows + last)
        far, above = slice(rows - last, rows - first), slice(ext_rows - last, ext_rows - first)
        return [
            send(ref.at[lead + (src, lanes)], ref.at[lead + (dst, lanes)], lat_send.at[2 * i + n], lat_recv.at[2 * i + n], at(dz=dz))
            for n, (src, dst, dz) in enumerate(((near, below, -1), (far, above, 1)))
        ]

    def send_strips(out, into, i):
        return [
            send(out.at[way], into.at[way, 0:rows], lon_send.at[2 * i + way], lon_recv.at[2 * i + way], at(dl=dl))
            for way, dl in ((0, 1), (1, -1))
        ]

    parts_sent = itertools.count()

    def send_part(src, dst):
        i = next(parts_sent)
        return send(src, dst, dep_send.at[i], dep_recv.at[i], at(dd=1))

    def send_deep(ref, i, part):
        return send_part(ref.at[(bottom_level - i,) + part], ref.at[(layers + i,) + part])

    def send_level(ref):
        return send_deep(ref, 0, whole)

    strips = send_strips(strips_out.at[0], strips_in.at[0], 0)
    first_rows = [
        send(rows_out.at[i], rows_in.at[i], lat_send.at[i], lat_recv.at[i], at(dz=dz)) for i, dz in ((0, -1), (1, 1))
    ]
    strips += send_strips(strips_out.at[1], strips_in.at[1], 1)
    last_rows = [
        send(
            fields.at[5, every, pl.ds(src, 1), inner[1]], edges.at[every, pl.ds(dst, 1), inner[1]],
            lat_send.at[2 + i], lat_recv.at[2 + i], at(dz=dz),
        )
        for i, (src, dst, dz) in enumerate(((0, 0, -1), (rows - 1, 2 * HALO - 1, 1)))
    ]
    first_level = [
        send_part(fields.at[(slice(0, 2), bottom_level) + inner], fields.at[(slice(0, 2), layers) + inner]),
        send_part(fields.at[(5, bottom_level) + inner], fields.at[(5, layers) + inner]),
        send_part(dz_out, dz_in),
    ]

    arrive(*strips)
    corners = send_rows(strips_in, (slice(0, 2), slice(0, 2)), slice(0, 128), 2)
    drag_rows = [
        send_rows(fields, (3, every), inner[1], 3, 0, 2),
        send_rows(fields, (4, every), inner[1], 4, 0, 2),
    ]
    flat_rows = send_rows(flat, (), slice(0, 128 + columns), 6)

    lane_x = lax.broadcasted_iota(jnp.int32, (ext_rows, 128), 1)
    even = (lane_x // HALO) % 2 == 0

    def combine(pair, part):
        from_left, from_right = pair[0, part], pair[1, part]
        return [jnp.where(even[part], from_right, from_left), jnp.where(even[part], from_left, from_right)]

    def unpack(both, slot):
        return pltpu.roll(both[slot % 2], (128 - HALO * slot) % 128, 1)

    one = lambda flag: jnp.where(flag, 1.0, 0.0).astype(jnp.float32)
    lane_mask = jnp.where(lane_x < HALO, one(lon < n_lon - 1), jnp.where(lane_x >= 128 - HALO, one(lon > 0), 0.0))
    row_8 = lax.broadcasted_iota(jnp.int32, (2 * HALO, ext_columns), 0)
    row_mask = jnp.where(row_8 < HALO, one(lat < n_lat - 1), one(lat > 0))
    couple = fields.at[0]

    def unpack_all(part):
        for m in range(2):
            both = combine(strips_in.at[m], part)
            for f in range(3):
                for j in range(layers):
                    halo = unpack(both, f * layers + j)
                    if m == 0 and f == 0:
                        halo = halo * lane_mask[part]
                        if part.start:
                            halo = halo * row_mask[:, columns:]
                    fields[3 * m + f, j, part, columns:] = halo
            if m == 0:
                flat[part, 128 + columns :] = unpack(both, 3 * layers)

    unpack_all(slice(0, rows))
    arrive(*first_rows)
    for f in range(3):
        for pair in range(layers // 2):
            from_next, from_previous = rows_in[0, f, pair], rows_in[1, f, pair]
            both = [
                jnp.where(upper, from_next, from_previous),
                pltpu.roll(jnp.where(upper, from_previous, from_next), HALO, 0),
            ]
            for odd in range(2):
                halo = both[odd] if f else both[odd] * row_mask[:, 0:columns]
                fields[f, 2 * pair + odd, rows:, 0:columns] = halo
    arrive(*last_rows)
    arrive(*first_level)

    tangents = [fields.at[1], tan1, tan2, tan3]
    drag = [fields.at[2 + s] for s in range(4)]

    def capacity_at(j, part):
        here = couple[(j,) + part]
        capacity[(j,) + part] = jnp.where(here > 0.0, 1.0, 0.0) - here * around(couple, None, j, part)

    def tangent_at(s, j, part):
        value = tangents[s]
        at_part = (j,) + part
        damp = drag[s][at_part]
        return couple[at_part] * around(couple, value, j, part) + (capacity[at_part] - damp * damp) * value[at_part]

    def zonal(block, j):
        weighted = block * flat[0:rows, 128 : 128 + columns]
        folded = weighted[:, 0:128]
        for part in range(1, columns // 128):
            folded = folded + weighted[:, 128 * part : 128 * part + 128]
        return jnp.sum(folded, axis=1, keepdims=True) * (level_dz[own(j)] * scale)

    tiles = rows // 8
    lane_8 = lax.broadcasted_iota(jnp.int32, (8, 128), 1)

    def put(sums, column, j):
        for t in range(tiles):
            sums = jnp.where(lane_8 == t * layers + j, column[8 * t : 8 * t + 8], sums)
        return sums

    def gather(f, sums):
        zone[f] = sums
        zones[f, lon] = sums
        return [
            send(zone.at[f], zones.at[f, lon + (n_lon if dd else 0)], zone_send.at[f, i], zone_recv.at[f, i], at(dl=dl, dd=dd))
            for i, (dl, dd) in enumerate(plane)
        ]

    last = drag[3]
    sums = jnp.zeros((8, 128), jnp.float32)
    for j in range(layers):
        capacity_at(j, inner)
    for j in range(layers):
        here = last[(j,) + inner]
        outer = jnp.concatenate([edges[j], jnp.zeros((2 * HALO, ext_columns - columns), jnp.float32)], axis=1)
        spread = jnp.concatenate([couple[j, 0:rows] * last[j, 0:rows], couple[j, rows:] * outer], axis=0)
        final = couple[(j,) + inner] * around(couple, last, j, inner, spread)
        final = final + (capacity[(j,) + inner] - here * here * (1.0 / 3.0)) * here
        sums = put(sums, zonal(final, j) * (1.0 / math.sqrt(3.0 * cubic_drag)), j)
    pl.semaphore_wait(ready, len(across))
    gathered_0 = gather(0, sums)
    drag_rows.append(send_rows(fields, (5, every), inner[1], 5, 0, 3))
    for j in range(layers):
        tan1[(j,) + inner] = tangent_at(0, j, inner)

    arrive(*corners)
    unpack_all(slice(rows, ext_rows))
    border = [
        send_part(fields.at[(slice(0, 2), bottom_level) + part], fields.at[(slice(0, 2), layers) + part])
        for part in frame
    ]
    for j in range(layers):
        if j == bottom_level:
            arrive(*border)
        for part in frame:
            capacity_at(j, part)
            tan1[(j,) + part] = tangent_at(0, j, part)
    pending = send_level(tan1)

    for s in (1, 2):
        nxt = tangents[s + 1]
        arrive(*drag_rows[s - 1])
        for j in range(layers):
            if j == bottom_level:
                arrive(pending)
            nxt[j] = tangent_at(s, j, whole)
        pending = send_level(nxt)

    pair = [jnp.zeros((rows, 128), jnp.float32)] * 2
    for j in range(layers):
        block = tan3[(j,) + inner]
        tan3_wide[(j,) + inner] = block
        pack(pair, block, j)
    strip3_out[0] = pair[0]
    strip3_out[1] = pair[1]
    strips = send_strips(strip3_out, strip3_in, 2)
    third_rows = send_rows(tan3_wide, (every,), inner[1], 7)

    sums = jnp.zeros((8, 128), jnp.float32)
    for j in range(layers):
        if j == bottom_level:
            arrive(pending)
        sums = put(sums, zonal(tangent_at(3, j, inner), j), j)
    gathered_1 = gather(1, sums)

    def collect(f):
        mine = zones[f, 0]
        other = zones[f, n_lon]
        for i in range(1, n_lon):
            mine = mine + zones[f, i]
            other = other + zones[f, n_lon + i]
        for t in range(tiles):
            shift = (128 - layers * t) % 128
            a = pltpu.roll(mine, shift, 1) if shift else mine
            b = pltpu.roll(other, (shift + layers) % 128, 1)
            totals[f, 8 * t : 8 * t + 8] = jnp.where(lane_8 < layers, a, b)
        return send_rows(totals, (f,), slice(0, 128), 8 + f)

    def prefix_rows(f, part):
        count = part.stop - part.start
        places = [k if k < layers else layers + all_layers - 1 - k for k in range(all_layers)]
        terms = [jnp.broadcast_to(totals[f, part, p : p + 1], (count, 128)) for p in places]
        stream = both_ways(terms, upright, False)
        prefix = both_ways([weights[k, part] * stream[k] for k in range(all_layers)], upright, True)
        for k in range(layers + DEEP):
            prefixes[f, k, part] = prefix[k]
        return stream

    arrive(*flat_rows, *drag_rows[2])
    deep = [send_deep(couple, i, whole) for i in range(1, DEEP)]
    deep += [send_deep(drag[3], 0, part) for part in frame]
    deep += [send_deep(drag[s], i, whole) for s, i in ((3, 1), (3, 2), (2, 0), (2, 1), (1, 0))]
    deep += [send_deep(tan2, 1, whole)]
    deep_third = [send_deep(tan3_wide, i, inner) for i in range(3)]
    for k in range(all_layers):
        weights[k] = jnp.broadcast_to(flat[:, k : k + 1], (ext_rows, 128))

    def start_adjoint(f, ref, part):
        basin = flat[part, 128:]
        for j in range(layers + DEEP):
            thick = level_dz[own(j)] * scale if j < layers else dz_in[j - layers : j - layers + 1, 0:1]
            ref[0, j, part] = basin * thick * jnp.concatenate([prefixes[f, j, part]] * (ext_columns // 128), axis=1)

    def adjoint_at(ref, n, j, part):
        at_part = (j,) + part
        damp = drag[3 - n][at_part]
        keep = capacity[at_part] - damp * damp
        return couple[at_part] * around(couple, ref.at[n], j, part) + keep * ref[(n,) + at_part], damp

    def lam_step(n):
        for j in range(layers + 3 - n):
            if n < 3:
                lam[n + 1, j] = adjoint_at(lam, n, j, whole)[0]
            else:
                grad[own(j)] = adjoint_at(lam, n, j, inner)[0]

    ratio = 6.0 * cubic_drag / math.sqrt(3.0 * cubic_drag)

    def mu_step(n, bands):
        tangent = tan3_wide if n == 0 else tangents[3 - n]
        for j in range(layers + 3 - n):
            for band in bands:
                part = (band, whole[1] if n < 3 else inner[1])
                new, damp = adjoint_at(mu, n, j, part)
                new = new - (ratio * damp) * (tangent[(j,) + part] * lam[(n, j) + part])
                if n < 3:
                    mu[(n + 1, j) + part] = new
                else:
                    hess[(own(j),) + part] = new

    arrive(*gathered_0)
    border = collect(0)
    streams = prefix_rows(0, inner[0])
    spots = lax.broadcasted_iota(jnp.int32, (rows, rows), 0) == lax.broadcasted_iota(jnp.int32, (rows, rows), 1)
    for j in range(layers):
        line = jnp.sum(jnp.where(spots, streams[j][:, 0:rows], 0.0), axis=0, keepdims=True)
        overturning[pl.ds(own(j), 1), :] = line
    arrive(*strips)
    corners = send_rows(strip3_in, (slice(0, 2),), slice(0, 128), 10)
    both = combine(strip3_in, inner[0])
    for j in range(layers):
        tan3_wide[(j,) + side] = unpack(both, j)
    deep_third += [send_deep(tan3_wide, i, side) for i in range(3)]
    arrive(*deep)
    for j in range(layers, layers + 3):
        capacity_at(j, whole)
    start_adjoint(0, lam, inner[0])
    arrive(*border)
    prefix_rows(0, bottom[0])
    start_adjoint(0, lam, bottom[0])
    lam_step(0)
    lam_step(1)

    arrive(*gathered_1)
    border = collect(1)
    prefix_rows(1, inner[0])
    start_adjoint(1, mu, inner[0])
    arrive(*deep_third)
    lam_step(2)
    for n in range(3):
        mu_step(n, [inner[0]])
    mu_step(3, [slice(8, rows - 8)])
    arrive(*third_rows, *corners)
    both = combine(strip3_in, bottom[0])
    for j in range(layers):
        tan3_wide[j, bottom[0], columns:] = unpack(both, j)
    deep_third = [send_deep(tan3_wide, i, bottom) for i in range(3)]
    lam_step(3)

    arrive(*border)
    prefix_rows(1, bottom[0])
    start_adjoint(1, mu, bottom[0])
    arrive(*deep_third)
    for n in range(3):
        mu_step(n, [slice(rows - 8, ext_rows), slice(0, 8)])
    mu_step(3, [slice(rows - 8, rows), slice(0, 8)])
    finish()


def both_ways(terms, upright, forward):
    count = len(terms)
    up = [terms[0]]
    for k in range(1, count):
        up.append(up[-1] + terms[k])
    down = [terms[-1]]
    for k in range(count - 2, -1, -1):
        down.append(down[-1] + terms[k])
    down = down[::-1]
    choose_up = upright if forward else jnp.logical_not(upright)
    return [jnp.where(choose_up, a, b) for a, b in zip(up, down)]


def store(hess, grad, overturning, hess_out, grad_out, overturning_out, sem):
    copies = [
        pltpu.make_async_copy(src, dst, sem.at[i])
        for i, (src, dst) in enumerate(((hess, hess_out), (grad, grad_out), (overturning, overturning_out)))
    ]
    for copy in copies:
        copy.start()
    for copy in copies:
        copy.wait()


def solution(mesh):
    n_lon, n_lat, n_depth = (mesh.shape[name] for name in ("lon", "lat", "depth"))

    def shards(states, direction, mixing, level_dz, lat_width, cost_weight, ocean_columns, atlantic, levels):
        layers, rows, columns = direction.shape
        ext = (rows + 2 * HALO, columns + 128)
        tall = (layers + DEEP,) + ext
        f32, i32 = jnp.float32, jnp.int32
        vmem = lambda *shape: pltpu.VMEM(shape, f32)
        dma = lambda count: pltpu.SemaphoreType.DMA((count,))
        in_vmem, in_hbm = (pl.BlockSpec(memory_space=m) for m in (pltpu.VMEM, pltpu.HBM))
        scale = 1.0 / math.sqrt(columns * n_lon * layers * n_depth)
        body = functools.partial(kernel, n_lon, n_lat, n_depth, scale, math.sqrt(columns * n_lon))
        results = pl.pallas_call(
            body,
            out_shape=(vmem(*direction.shape), vmem(*direction.shape), vmem(layers, rows)),
            in_specs=[in_hbm] * 9,
            out_specs=(in_vmem,) * 3,
            scratch_shapes=[
                vmem(*states.shape), vmem(*direction.shape), vmem(*direction.shape),
                pltpu.VMEM((rows, columns), i32), pltpu.VMEM((rows, columns), i32), pltpu.VMEM((rows, columns), i32),
                vmem(*cost_weight.shape), pltpu.SMEM(level_dz.shape, f32), pltpu.SMEM(lat_width.shape, f32),
                vmem(6, *tall), vmem(layers + 3, *ext), vmem(*tall), vmem(*tall), vmem(*tall),
                vmem(*tall), vmem(4, *tall), vmem(4, *tall),
                vmem(ext[0], 128 + ext[1]), vmem(layers, 2 * HALO, columns),
                vmem(2, 3, layers // 2, 2 * HALO, columns), vmem(2, 3, layers // 2, 2 * HALO, columns),
                vmem(2, 2, rows, 128), vmem(2, 2, ext[0], 128),
                vmem(2, rows, 128), vmem(2, ext[0], 128), vmem(8, 128), vmem(8, 128),
                vmem(2, 8, 128), vmem(2, 2 * n_lon, 8, 128), vmem(2, ext[0], 128),
                vmem(2, layers + DEEP, ext[0], 128), vmem(n_depth * layers, ext[0], 128),
                dma(9), dma(22), dma(22), dma(6), dma(6), dma(28), dma(28),
                pltpu.SemaphoreType.DMA((2, 2 * n_lon - 1)), pltpu.SemaphoreType.DMA((2, 2 * n_lon - 1)),
                pltpu.SemaphoreType.REGULAR,
            ],
            compiler_params=pltpu.CompilerParams(
                collective_id=0, has_side_effects=True, vmem_limit_bytes=48 * 2**20
            ),
            cost_estimate=pl.CostEstimate(flops=3 * 10**7, bytes_accessed=3 * 10**6, transcendentals=0),
        )(*(
            pltpu.with_memory_space_constraint(x, pltpu.HBM)
            for x in (states, direction, mixing, level_dz, lat_width, cost_weight, ocean_columns, atlantic, levels)
        ))
        return pl.pallas_call(
            store,
            out_shape=tuple(jax.ShapeDtypeStruct(result.shape, f32) for result in results),
            in_specs=[in_vmem] * 3,
            out_specs=(in_hbm,) * 3,
            scratch_shapes=[dma(3)],
            cost_estimate=pl.CostEstimate(flops=0, bytes_accessed=10**6, transcendentals=0),
        )(*(pltpu.with_memory_space_constraint(result, pltpu.VMEM) for result in results))

    placed = (
        P(None, "depth", "lat", "lon"),
        P("depth", "lat", "lon"),
        P("depth", "lat", "lon"),
        P("depth"),
        P("lat"),
        P(None, "lat"),
        P("lat", "lon"),
        P("lat", "lon"),
        P("lat", "lon"),
    )
    return jax.shard_map(
        shards,
        mesh=mesh,
        in_specs=placed,
        out_specs=(P("depth", "lat", "lon"), P("depth", "lat", "lon"), P("depth", "lat")),
        check_vma=False,
    )
```

```python
import functools
import itertools
import math

import jax
import jax.numpy as jnp
from jax import lax
from jax.experimental import pallas as pl
from jax.experimental.pallas import tpu as pltpu
from jax.sharding import PartitionSpec as P

MESH = pl.DeviceIdType.MESH
diffusion_step = 0.08
cubic_drag = 0.15

HALO = 4
LINE = 4
DEEP = 4


def around(couple, value, level, part, here=None):
    if here is None:
        here = couple[level] if value is None else couple[level] * value[level]
    rows, columns = here.shape
    total = pltpu.roll(here, 1, 1) + pltpu.roll(here, columns - 1, 1)
    total = (total + (pltpu.roll(here, 1, 0) + pltpu.roll(here, rows - 1, 0)))[part]
    for k in (level - 1, level + 1):
        if k >= 0:
            there = couple[(k,) + part]
            total = total + (there if value is None else there * value[(k,) + part])
    return total


def kernel(
    n_lon, n_lat, n_depth, scale, grid_scale,
    states, direction, mixing, dz_in_hbm, width_in_hbm, weight_in_hbm, ocean, atlantic, levels_in,
    hess, grad, overturning,
    st_states, st_dir, st_mix, st_ocean, st_atl, st_lev, cost_weight, level_dz, lat_width,
    fields, capacity, tan1, tan2, tan3, tan3_wide, lam, mu,
    flat, edges, rows_out, rows_in, strips_out, strips_in, strip3_out, strip3_in, dz_out, dz_in, zone, zones, totals, prefixes, weights,
    in_sem, lat_send, lat_recv, lon_send, lon_recv, dep_send, dep_recv, zone_send, zone_recv, ready,
):
    layers, rows, columns = direction.shape
    all_layers = 2 * layers
    ext_rows, ext_columns = fields.shape[-2:]
    lon, lat, dep = lax.axis_index("lon"), lax.axis_index("lat"), lax.axis_index("depth")
    wrap = lambda value, size: lax.rem(value + size, size)

    def at(dl=0, dz=0, dd=0):
        return (wrap(lon + dl, n_lon), wrap(lat + dz, n_lat), wrap(dep + dd, n_depth))

    lines = n_lon // LINE
    plane = [(i, k, d) for i in range(lines) for k in range(LINE) for d in range(n_depth) if i or k or d]
    plane.sort(key=lambda offset: not (offset[0] and offset[1]))
    start = lon // LINE * LINE
    in_line = lambda i: lax.rem(lon - start + i, LINE)
    across = [at(dl=LINE * i) for i in range(1, lines)]
    peers = [
        (start + in_line(i), lat, wrap(dep + d, n_depth))
        for d in range(n_depth) for i in range(LINE) if i or d
    ]
    peers += across + [at(dl=i) for i in (1, -1)] + [at(dz=z) for z in (1, -1)]
    barrier = pltpu.get_barrier_semaphore()
    for peer in peers:
        pl.semaphore_signal(barrier, inc=1, device_id=peer, device_id_type=MESH)

    loads = [
        pltpu.make_async_copy(src, dst, in_sem.at[i])
        for i, (src, dst) in enumerate((
            (width_in_hbm, lat_width), (weight_in_hbm, cost_weight), (dz_in_hbm, level_dz), (levels_in, st_lev),
            (ocean, st_ocean), (atlantic, st_atl), (mixing, st_mix), (direction, st_dir), (states, st_states),
        ))
    ]
    for load in loads:
        load.start()

    sends, expected = [], {}

    def send(src, dst, send_sem, recv_sem, device):
        copy = pltpu.make_async_remote_copy(
            src_ref=src, dst_ref=dst, send_sem=send_sem, recv_sem=recv_sem, device_id=device, device_id_type=MESH
        )
        copy.start()
        sends.append(copy)
        expected[id(copy)] = copy
        return copy

    def arrive(*copies):
        for copy in copies:
            expected.pop(id(copy)).wait_recv()

    def finish():
        for copy in list(expected.values()):
            arrive(copy)
        for copy in sends:
            copy.wait_send()

    upright = dep == 0
    own = lambda j: jnp.where(upright, j, layers - 1 - j)
    lane = lax.broadcasted_iota(jnp.int32, (rows, 128), 1)
    group = lane // HALO
    row = lax.broadcasted_iota(jnp.int32, (rows, 128), 0)

    for load in loads[:3]:
        load.wait()
    width = jnp.zeros((rows, 128), jnp.float32)
    for r in range(rows):
        width = jnp.where(row == r, lat_width[r], width)
    square_row = lax.broadcasted_iota(jnp.int32, (rows, rows), 0)
    square_lane = lax.broadcasted_iota(jnp.int32, (rows, rows), 1)
    by_level = jnp.zeros((rows, 128), jnp.float32)
    for k in range(all_layers):
        line = cost_weight[pl.ds(jnp.where(upright, k, all_layers - 1 - k), 1), :]
        column = jnp.sum(jnp.where(square_row == square_lane, line, 0.0), axis=1, keepdims=True)
        by_level = jnp.where(lane == k, column * grid_scale, by_level)
    flat[0:rows, 0:128] = by_level
    thick = jnp.zeros(dz_out.shape, jnp.float32)
    for i in range(DEEP):
        thick = jnp.where(lax.broadcasted_iota(jnp.int32, dz_out.shape, 0) == i, level_dz[own(layers - 1 - i)] * scale, thick)
    dz_out[...] = thick

    for load in loads[3:]:
        load.wait()
    basin = st_atl[...].astype(jnp.float32) * jnp.concatenate([width] * (columns // 128), axis=1)
    flat[0:rows, 128 : 128 + columns] = basin
    reach = st_lev[...] * st_ocean[...]

    edge = columns - 128
    packed = [[jnp.zeros((rows, 128), jnp.float32)] * 2 for _ in range(2)]

    def pack(pair, block, slot):
        right = pltpu.roll(block[:, edge:], (HALO * slot) % 128, 1)
        left = pltpu.roll(block[:, :128], (HALO * slot) % 128, 1)
        pair[0] = jnp.where(group == (slot - 1) % 32, right, pair[0])
        pair[1] = jnp.where(group == slot, left, pair[1])

    pack(packed[0], basin, 3 * layers)
    upper = lax.broadcasted_iota(jnp.int32, (2 * HALO, columns), 0) < HALO
    held = None
    for j in range(layers):
        k = own(j)
        wet = dep * layers + k < reach
        couple = jnp.where(wet, math.sqrt(diffusion_step) * st_mix[k], 0.0)
        parts = [couple, st_dir[k]]
        parts += [jnp.where(wet, math.sqrt(3.0 * cubic_drag) * st_states[s, k], 0.0) for s in range(4)]
        for f, part in enumerate(parts):
            fields[f, j, 0:rows, 0:columns] = part
            pack(packed[f // 3], part, (f % 3) * layers + j)
            if f < 3 and j % 2:
                before, after = held[f][0 : 2 * HALO], pltpu.roll(part[0 : 2 * HALO], HALO, 0)
                rows_out[0, f, j // 2] = jnp.where(upper, before, after)
                before, after = held[f][rows - 2 * HALO :], pltpu.roll(part[rows - 2 * HALO :], HALO, 0)
                rows_out[1, f, j // 2] = jnp.where(upper, after, before)
        held = parts
    for m in range(2):
        for way in range(2):
            strips_out[m, way] = packed[m][way]

    pl.semaphore_wait(barrier, len(peers))
    for peer in across:
        pl.semaphore_signal(ready, inc=1, device_id=peer, device_id_type=MESH)

    every = slice(0, layers)
    inner = (slice(0, rows), slice(0, columns))
    bottom = (slice(rows, ext_rows), slice(0, ext_columns))
    side = (slice(0, rows), slice(columns, ext_columns))
    frame = (bottom, side)
    whole = (slice(0, ext_rows), slice(0, ext_columns))
    bottom_level = layers - 1

    def send_rows(ref, lead, lanes, i, first=0, last=HALO):
        near, below = slice(first, last), slice(rows + first, rows + last)
        far, above = slice(rows - last, rows - first), slice(ext_rows - last, ext_rows - first)
        return [
            send(ref.at[lead + (src, lanes)], ref.at[lead + (dst, lanes)], lat_send.at[2 * i + n], lat_recv.at[2 * i + n], at(dz=dz))
            for n, (src, dst, dz) in enumerate(((near, below, -1), (far, above, 1)))
        ]

    def send_strips(out, into, i):
        return [
            send(out.at[way], into.at[way, 0:rows], lon_send.at[2 * i + way], lon_recv.at[2 * i + way], at(dl=dl))
            for way, dl in ((0, 1), (1, -1))
        ]

    parts_sent = itertools.count()

    def send_part(src, dst):
        i = next(parts_sent)
        return send(src, dst, dep_send.at[i], dep_recv.at[i], at(dd=1))

    def send_deep(ref, i, part):
        return send_part(ref.at[(bottom_level - i,) + part], ref.at[(layers + i,) + part])

    def send_level(ref):
        return send_deep(ref, 0, whole)

    strips = send_strips(strips_out.at[0], strips_in.at[0], 0)
    first_rows = [
        send(rows_out.at[i], rows_in.at[i], lat_send.at[i], lat_recv.at[i], at(dz=dz)) for i, dz in ((0, -1), (1, 1))
    ]
    strips += send_strips(strips_out.at[1], strips_in.at[1], 1)
    last_rows = [
        send(
            fields.at[5, every, pl.ds(src, 1), inner[1]], edges.at[every, pl.ds(dst, 1), inner[1]],
            lat_send.at[2 + i], lat_recv.at[2 + i], at(dz=dz),
        )
        for i, (src, dst, dz) in enumerate(((0, 0, -1), (rows - 1, 2 * HALO - 1, 1)))
    ]
    first_level = [
        send_part(fields.at[(slice(0, 2), bottom_level) + inner], fields.at[(slice(0, 2), layers) + inner]),
        send_part(fields.at[(5, bottom_level) + inner], fields.at[(5, layers) + inner]),
        send_part(dz_out, dz_in),
    ]

    arrive(*strips)
    corners = send_rows(strips_in, (slice(0, 2), slice(0, 2)), slice(0, 128), 2)
    drag_rows = [
        send_rows(fields, (3, every), inner[1], 3, 0, 2),
        send_rows(fields, (4, every), inner[1], 4, 0, 2),
    ]
    flat_rows = send_rows(flat, (), slice(0, 128 + columns), 6)

    lane_x = lax.broadcasted_iota(jnp.int32, (ext_rows, 128), 1)
    even = (lane_x // HALO) % 2 == 0

    def combine(pair, part):
        from_left, from_right = pair[0, part], pair[1, part]
        return [jnp.where(even[part], from_right, from_left), jnp.where(even[part], from_left, from_right)]

    def unpack(both, slot):
        return pltpu.roll(both[slot % 2], (128 - HALO * slot) % 128, 1)

    one = lambda flag: jnp.where(flag, 1.0, 0.0).astype(jnp.float32)
    lane_mask = jnp.where(lane_x < HALO, one(lon < n_lon - 1), jnp.where(lane_x >= 128 - HALO, one(lon > 0), 0.0))
    row_8 = lax.broadcasted_iota(jnp.int32, (2 * HALO, ext_columns), 0)
    row_mask = jnp.where(row_8 < HALO, one(lat < n_lat - 1), one(lat > 0))
    couple = fields.at[0]

    def unpack_all(part):
        for m in range(2):
            both = combine(strips_in.at[m], part)
            for f in range(3):
                for j in range(layers):
                    halo = unpack(both, f * layers + j)
                    if m == 0 and f == 0:
                        halo = halo * lane_mask[part]
                        if part.start:
                            halo = halo * row_mask[:, columns:]
                    fields[3 * m + f, j, part, columns:] = halo
            if m == 0:
                flat[part, 128 + columns :] = unpack(both, 3 * layers)

    unpack_all(slice(0, rows))
    arrive(*first_rows)
    for f in range(3):
        for pair in range(layers // 2):
            from_next, from_previous = rows_in[0, f, pair], rows_in[1, f, pair]
            both = [
                jnp.where(upper, from_next, from_previous),
                pltpu.roll(jnp.where(upper, from_previous, from_next), HALO, 0),
            ]
            for odd in range(2):
                halo = both[odd] if f else both[odd] * row_mask[:, 0:columns]
                fields[f, 2 * pair + odd, rows:, 0:columns] = halo
    arrive(*last_rows)
    arrive(*first_level)

    tangents = [fields.at[1], tan1, tan2, tan3]
    drag = [fields.at[2 + s] for s in range(4)]

    def capacity_at(j, part):
        here = couple[(j,) + part]
        capacity[(j,) + part] = jnp.where(here > 0.0, 1.0, 0.0) - here * around(couple, None, j, part)

    def tangent_at(s, j, part):
        value = tangents[s]
        at_part = (j,) + part
        damp = drag[s][at_part]
        return couple[at_part] * around(couple, value, j, part) + (capacity[at_part] - damp * damp) * value[at_part]

    def zonal(block, j):
        weighted = block * flat[0:rows, 128 : 128 + columns]
        folded = weighted[:, 0:128]
        for part in range(1, columns // 128):
            folded = folded + weighted[:, 128 * part : 128 * part + 128]
        return jnp.sum(folded, axis=1, keepdims=True) * (level_dz[own(j)] * scale)

    tiles = rows // 8
    lane_8 = lax.broadcasted_iota(jnp.int32, (8, 128), 1)

    def put(sums, column, j):
        for t in range(tiles):
            sums = jnp.where(lane_8 == t * layers + j, column[8 * t : 8 * t + 8], sums)
        return sums

    def gather(f, sums):
        zone[f] = sums
        zones[f, lon] = sums
        copies = []
        for n, (i, k, d) in enumerate(plane):
            device = (wrap(start + LINE * i, n_lon) + in_line(k), lat, wrap(dep + d, n_depth))
            slot = lon + (n_lon if d else 0)
            copies.append(send(zone.at[f], zones.at[f, slot], zone_send.at[f, n], zone_recv.at[f, n], device))
        return copies

    last = drag[3]
    sums = jnp.zeros((8, 128), jnp.float32)
    for j in range(layers):
        capacity_at(j, inner)
    for j in range(layers):
        here = last[(j,) + inner]
        outer = jnp.concatenate([edges[j], jnp.zeros((2 * HALO, ext_columns - columns), jnp.float32)], axis=1)
        spread = jnp.concatenate([couple[j, 0:rows] * last[j, 0:rows], couple[j, rows:] * outer], axis=0)
        final = couple[(j,) + inner] * around(couple, last, j, inner, spread)
        final = final + (capacity[(j,) + inner] - here * here * (1.0 / 3.0)) * here
        sums = put(sums, zonal(final, j) * (1.0 / math.sqrt(3.0 * cubic_drag)), j)
    pl.semaphore_wait(ready, len(across))
    gathered_0 = gather(0, sums)
    drag_rows.append(send_rows(fields, (5, every), inner[1], 5, 0, 3))
    for j in range(layers):
        tan1[(j,) + inner] = tangent_at(0, j, inner)

    arrive(*corners)
    unpack_all(slice(rows, ext_rows))
    border = [
        send_part(fields.at[(slice(0, 2), bottom_level) + part], fields.at[(slice(0, 2), layers) + part])
        for part in frame
    ]
    for j in range(layers):
        if j == bottom_level:
            arrive(*border)
        for part in frame:
            capacity_at(j, part)
            tan1[(j,) + part] = tangent_at(0, j, part)
    pending = send_level(tan1)
    deep = [send_deep(couple, i, whole) for i in (1, 2)]

    for s in (1, 2):
        nxt = tangents[s + 1]
        arrive(*drag_rows[s - 1])
        for j in range(layers):
            if j == bottom_level:
                arrive(pending)
            nxt[j] = tangent_at(s, j, whole)
        pending = send_level(nxt)
        if s == 1:
            deep += [send_deep(couple, 3, whole), send_deep(drag[1], 0, whole)]
    arrive(*drag_rows[2])
    deep += [send_deep(drag[3], 0, part) for part in frame]
    deep += [send_deep(drag[t], i, whole) for t, i in ((3, 1), (3, 2), (2, 0), (2, 1))]
    deep += [send_deep(tan2, 1, whole)]

    def collect(f):
        mine = zones[f, 0]
        other = zones[f, n_lon]
        for i in range(1, n_lon):
            mine = mine + zones[f, i]
            other = other + zones[f, n_lon + i]
        for t in range(tiles):
            shift = (128 - layers * t) % 128
            a = pltpu.roll(mine, shift, 1) if shift else mine
            b = pltpu.roll(other, (shift + layers) % 128, 1)
            totals[f, 8 * t : 8 * t + 8] = jnp.where(lane_8 < layers, a, b)
        return send_rows(totals, (f,), slice(0, 128), 8 + f)

    def prefix_rows(f, part):
        count = part.stop - part.start
        places = [k if k < layers else layers + all_layers - 1 - k for k in range(all_layers)]
        terms = [jnp.broadcast_to(totals[f, part, p : p + 1], (count, 128)) for p in places]
        stream = both_ways(terms, upright, False)
        prefix = both_ways([weights[k, part] * stream[k] for k in range(all_layers)], upright, True)
        for k in range(layers + DEEP):
            prefixes[f, k, part] = prefix[k]
        return stream

    sums = jnp.zeros((8, 128), jnp.float32)
    for j in range(layers - 1):
        sums = put(sums, zonal(tangent_at(3, j, inner), j), j)
    pair = [jnp.zeros((rows, 128), jnp.float32)] * 2
    for j in range(layers):
        block = tan3[(j,) + inner]
        tan3_wide[(j,) + inner] = block
        pack(pair, block, j)
    strip3_out[0] = pair[0]
    strip3_out[1] = pair[1]
    strips = send_strips(strip3_out, strip3_in, 2)
    third_rows = send_rows(tan3_wide, (every,), inner[1], 7)
    deep_third = [send_deep(tan3_wide, i, inner) for i in range(3)]
    for way, dl in ((0, 1), (1, -1)):
        for n, (src, dst, dz) in enumerate((
            (slice(0, HALO), slice(rows, rows + HALO), -1), (slice(rows - HALO, rows), slice(rows + HALO, ext_rows), 1)
        )):
            i = 4 + 2 * way + n
            third_rows.append(send(
                strip3_out.at[way, src], strip3_in.at[way, dst], lon_send.at[i + 2], lon_recv.at[i + 2], at(dl=dl, dz=dz)
            ))

    arrive(pending)
    sums = put(sums, zonal(tangent_at(3, bottom_level, inner), bottom_level), bottom_level)
    gathered_1 = gather(1, sums)
    arrive(*gathered_0)
    totals_0 = collect(0)

    arrive(*flat_rows)
    for k in range(all_layers):
        weights[k] = jnp.broadcast_to(flat[:, k : k + 1], (ext_rows, 128))

    def start_adjoint(f, ref, part):
        basin = flat[part, 128:]
        for j in range(layers + DEEP):
            thick = level_dz[own(j)] * scale if j < layers else dz_in[j - layers : j - layers + 1, 0:1]
            ref[0, j, part] = basin * thick * jnp.concatenate([prefixes[f, j, part]] * (ext_columns // 128), axis=1)

    def adjoint_at(ref, n, j, part):
        at_part = (j,) + part
        damp = drag[3 - n][at_part]
        keep = capacity[at_part] - damp * damp
        return couple[at_part] * around(couple, ref.at[n], j, part) + keep * ref[(n,) + at_part], damp

    def lam_step(n, bands):
        for j in range(layers + 3 - n):
            for band in bands:
                part = (band, whole[1] if n < 3 else inner[1])
                new = adjoint_at(lam, n, j, part)[0]
                if n < 3:
                    lam[(n + 1, j) + part] = new
                else:
                    grad[(own(j),) + part] = new

    ratio = 6.0 * cubic_drag / math.sqrt(3.0 * cubic_drag)

    def mu_step(n, bands):
        tangent = tan3_wide if n == 0 else tangents[3 - n]
        for j in range(layers + 3 - n):
            for band in bands:
                part = (band, whole[1] if n < 3 else inner[1])
                new, damp = adjoint_at(mu, n, j, part)
                new = new - (ratio * damp) * (tangent[(j,) + part] * lam[(n, j) + part])
                if n < 3:
                    mu[(n + 1, j) + part] = new
                else:
                    hess[(own(j),) + part] = new

    streams = prefix_rows(0, inner[0])
    spots = lax.broadcasted_iota(jnp.int32, (rows, rows), 0) == lax.broadcasted_iota(jnp.int32, (rows, rows), 1)
    for j in range(layers):
        line = jnp.sum(jnp.where(spots, streams[j][:, 0:rows], 0.0), axis=0, keepdims=True)
        overturning[pl.ds(own(j), 1), :] = line
    arrive(*deep)
    for j in range(layers, layers + 3):
        capacity_at(j, whole)
    start_adjoint(0, lam, inner[0])
    for n in range(3):
        lam_step(n, [inner[0]])
    lam_step(3, [slice(8, rows - 8)])
    arrive(*strips)
    both = combine(strip3_in, inner[0])
    for j in range(layers):
        tan3_wide[(j,) + side] = unpack(both, j)
    deep_third += [send_deep(tan3_wide, i, side) for i in range(3)]

    arrive(*gathered_1)
    border = collect(1)
    prefix_rows(1, inner[0])
    start_adjoint(1, mu, inner[0])
    arrive(*deep_third, *third_rows)
    both = combine(strip3_in, bottom[0])
    for j in range(layers):
        tan3_wide[j, bottom[0], columns:] = unpack(both, j)
    deep_third = [send_deep(tan3_wide, i, bottom) for i in range(3)]
    arrive(*totals_0)
    prefix_rows(0, bottom[0])
    start_adjoint(0, lam, bottom[0])
    for n in range(3):
        lam_step(n, [slice(rows - 8, ext_rows), slice(0, 8)])
    lam_step(3, [slice(rows - 8, rows), slice(0, 8)])

    arrive(*border)
    prefix_rows(1, bottom[0])
    start_adjoint(1, mu, bottom[0])
    arrive(*deep_third)
    for n in range(3):
        mu_step(n, [whole[0]])
    mu_step(3, [inner[0]])
    finish()


def both_ways(terms, upright, forward):
    count = len(terms)
    up = [terms[0]]
    for k in range(1, count):
        up.append(up[-1] + terms[k])
    down = [terms[-1]]
    for k in range(count - 2, -1, -1):
        down.append(down[-1] + terms[k])
    down = down[::-1]
    choose_up = upright if forward else jnp.logical_not(upright)
    return [jnp.where(choose_up, a, b) for a, b in zip(up, down)]


def store(hess, grad, overturning, hess_out, grad_out, overturning_out, sem):
    copies = [
        pltpu.make_async_copy(src, dst, sem.at[i])
        for i, (src, dst) in enumerate(((hess, hess_out), (grad, grad_out), (overturning, overturning_out)))
    ]
    for copy in copies:
        copy.start()
    for copy in copies:
        copy.wait()


def solution(mesh):
    n_lon, n_lat, n_depth = (mesh.shape[name] for name in ("lon", "lat", "depth"))

    def shards(states, direction, mixing, level_dz, lat_width, cost_weight, ocean_columns, atlantic, levels):
        layers, rows, columns = direction.shape
        ext = (rows + 2 * HALO, columns + 128)
        tall = (layers + DEEP,) + ext
        f32, i32 = jnp.float32, jnp.int32
        vmem = lambda *shape: pltpu.VMEM(shape, f32)
        dma = lambda count: pltpu.SemaphoreType.DMA((count,))
        in_vmem, in_hbm = (pl.BlockSpec(memory_space=m) for m in (pltpu.VMEM, pltpu.HBM))
        scale = 1.0 / math.sqrt(columns * n_lon * layers * n_depth)
        body = functools.partial(kernel, n_lon, n_lat, n_depth, scale, math.sqrt(columns * n_lon))
        results = pl.pallas_call(
            body,
            out_shape=(vmem(*direction.shape), vmem(*direction.shape), vmem(layers, rows)),
            in_specs=[in_hbm] * 9,
            out_specs=(in_vmem,) * 3,
            scratch_shapes=[
                vmem(*states.shape), vmem(*direction.shape), vmem(*direction.shape),
                pltpu.VMEM((rows, columns), i32), pltpu.VMEM((rows, columns), i32), pltpu.VMEM((rows, columns), i32),
                vmem(*cost_weight.shape), pltpu.SMEM(level_dz.shape, f32), pltpu.SMEM(lat_width.shape, f32),
                vmem(6, *tall), vmem(layers + 3, *ext), vmem(*tall), vmem(*tall), vmem(*tall),
                vmem(*tall), vmem(4, *tall), vmem(4, *tall),
                vmem(ext[0], 128 + ext[1]), vmem(layers, 2 * HALO, columns),
                vmem(2, 3, layers // 2, 2 * HALO, columns), vmem(2, 3, layers // 2, 2 * HALO, columns),
                vmem(2, 2, rows, 128), vmem(2, 2, ext[0], 128),
                vmem(2, rows, 128), vmem(2, ext[0], 128), vmem(8, 128), vmem(8, 128),
                vmem(2, 8, 128), vmem(2, 2 * n_lon, 8, 128), vmem(2, ext[0], 128),
                vmem(2, layers + DEEP, ext[0], 128), vmem(n_depth * layers, ext[0], 128),
                dma(9), dma(20), dma(20), dma(10), dma(10), dma(28), dma(28),
                pltpu.SemaphoreType.DMA((2, 2 * n_lon - 1)), pltpu.SemaphoreType.DMA((2, 2 * n_lon - 1)),
                pltpu.SemaphoreType.REGULAR,
            ],
            compiler_params=pltpu.CompilerParams(
                collective_id=0, has_side_effects=True, vmem_limit_bytes=48 * 2**20
            ),
            cost_estimate=pl.CostEstimate(flops=3 * 10**7, bytes_accessed=3 * 10**6, transcendentals=0),
        )(*(
            pltpu.with_memory_space_constraint(x, pltpu.HBM)
            for x in (states, direction, mixing, level_dz, lat_width, cost_weight, ocean_columns, atlantic, levels)
        ))
        return pl.pallas_call(
            store,
            out_shape=tuple(jax.ShapeDtypeStruct(result.shape, f32) for result in results),
            in_specs=[in_vmem] * 3,
            out_specs=(in_hbm,) * 3,
            scratch_shapes=[dma(3)],
            cost_estimate=pl.CostEstimate(flops=0, bytes_accessed=10**6, transcendentals=0),
        )(*(pltpu.with_memory_space_constraint(result, pltpu.VMEM) for result in results))

    placed = (
        P(None, "depth", "lat", "lon"),
        P("depth", "lat", "lon"),
        P("depth", "lat", "lon"),
        P("depth"),
        P("lat"),
        P(None, "lat"),
        P("lat", "lon"),
        P("lat", "lon"),
        P("lat", "lon"),
    )
    return jax.shard_map(
        shards,
        mesh=mesh,
        in_specs=placed,
        out_specs=(P("depth", "lat", "lon"), P("depth", "lat", "lon"), P("depth", "lat")),
        check_vma=False,
    )
```
